32 devices in a mesh: ctx: 16 (over z, x, core), head: 2 (over y).
Axes of the slice: x: 2, y: 2, z: 4, core: 2. Of those that a mesh axis runs over, the one named last changes fastest.
Arguments:
- queries: bfloat16 [4096, 4096], P(('ctx', 'head')), may hold values from -6 to 6
- keys: bfloat16 [4096, 1024], P(('ctx', 'head')), may hold values from -6 to 6
- values: bfloat16 [4096, 1024], P(('ctx', 'head')), may hold values from -1.5 to 1.5
- out_grad: bfloat16 [4096, 4096], P(('ctx', 'head')), may hold values from -6 to 6
- log_norm: float32 [4096, 32], P(('ctx', 'head')), may hold values from 2 to 4
- row_delta: float32 [4096, 32], P(('ctx', 'head')), may hold values from -10 to 10
- tile_pairs: int32 [16, 4, 4, 2], P('ctx'), may hold values from 0 to 1, as said below
- pair_count: int32 [16, 4], P('ctx'), may hold values from 0 to 4, as said below
Outputs:
- query_grad: bfloat16 [4096, 4096], P(('ctx', 'head'))
- key_grad: bfloat16 [4096, 1024], P(('ctx', 'head'))
- value_grad: bfloat16 [4096, 1024], P(('ctx', 'head'))
The draws below stay inside these ranges and needn't reach their ends.
Inputs may be any that keep to these rules, and one draw needn't show every extreme that they name: `tile_pairs`: Entries past pair_count are not read.
All inputs are finite; a program needn't handle non-finite values.
Results may differ from the reference program's by a relative error of at most 0.005.
Values may be sent and summed in bfloat16 or wider, within the bound.
No kernel may reach another device: no remote copies, remote signals or barrier semaphores. Data moves between devices by JAX's collectives and lax.ppermute only.
A program may use at most 64 MiB of HBM per device.

```python
import jax
import jax.numpy as jnp
from jax import lax

HEAD_DIM = 128
Q_HEADS = 32
KV_HEADS = 8
TILE = 128
WIN = 4
BLOCK = 256
TPB = 2
LIST_SLOTS = 4
SEQ = 4096
N_CTX = 16


def list_structure(key):
    all_pairs = TPB * TPB
    pair_index = jnp.arange(all_pairs, dtype=jnp.int32)
    query_part = pair_index // TPB
    key_part = pair_index % TPB
    lower_total = TPB * (TPB - 1) // 2
    extra_most = min(TPB, lower_total)
    base_key = jax.random.fold_in(key, 17)

    def one_list(block, cycle_step):
        list_key = jax.random.fold_in(base_key, block * WIN + cycle_step)
        key_perm, key_count, key_extra = jax.random.split(list_key, 3)
        ranks = jax.random.permutation(key_perm, all_pairs).astype(jnp.int32)
        level = jnp.where(query_part == key_part, 0, jnp.where(key_part < query_part, 1, 2)).astype(jnp.int32)
        first_key = level * all_pairs + ranks
        sort_key = jnp.where(cycle_step == 0, first_key, ranks)
        ordering = jnp.argsort(sort_key)[:LIST_SLOTS].astype(jnp.int32)
        later_count = jax.random.randint(key_count, (), 0, LIST_SLOTS + 1)
        later_count = jnp.where((block == WIN) & (cycle_step == 1), LIST_SLOTS, later_count)
        later_count = jnp.where(block == cycle_step, LIST_SLOTS, later_count)
        later_count = jnp.where(block < cycle_step, 0, later_count)
        first_count = TPB + jax.random.randint(key_extra, (), 0, extra_most + 1)
        count = jnp.where(cycle_step == 0, first_count, later_count).astype(jnp.int32)
        pairs = jnp.stack([ordering // TPB, ordering % TPB], axis=-1).astype(jnp.int32)
        return (pairs, count)
    blocks = jnp.arange(N_CTX, dtype=jnp.int32)
    cycle_steps = jnp.arange(WIN, dtype=jnp.int32)
    per_step = jax.vmap(one_list, in_axes=(None, 0))
    return jax.vmap(per_step, in_axes=(0, None))(blocks, cycle_steps)


def draw_tile_pairs(key, part):
    return list_structure(key)[0]


def draw_pair_count(key, part):
    return list_structure(key)[1]


def block_scale(key, dims, shards, least, high):
    factor_of = 1.0
    for axis_at, blocks in shards:
        draws = jax.random.uniform(jax.random.fold_in(jax.random.fold_in(key, 6), axis_at), (blocks,), jnp.float32, least / len(shards), high / len(shards))
        factor_of = factor_of * jnp.repeat(jnp.exp(draws), dims[axis_at] // blocks).reshape((-1,) + (1,) * (len(dims) - 1 - axis_at))
    return factor_of


def scatter_about(rng, shape, width, bound, cuts=(), kind=jnp.bfloat16):
    entries = jax.random.normal(rng, shape, jnp.float32) * width
    if len(cuts) > 0:
        entries = block_scale(rng, shape, cuts, -0.22, 0.18) * entries
    return jnp.clip(entries, min=-bound, max=bound).astype(kind)


def setup_inputs(seed: int = 0) -> dict:
    seeds = jax.random.split(jax.random.key(seed), 9)
    return {
        "queries": scatter_about(seeds[0], (SEQ, Q_HEADS * HEAD_DIM), 1.0, 6.0, ((0, 32),)),
        "keys": scatter_about(seeds[1], (SEQ, KV_HEADS * HEAD_DIM), 1.0, 6.0, ((0, 32),)),
        "values": scatter_about(seeds[2], (SEQ, KV_HEADS * HEAD_DIM), 0.25, 1.5, ((0, 32),)),
        "out_grad": scatter_about(seeds[3], (SEQ, Q_HEADS * HEAD_DIM), 1.0, 6.0, ((0, 32),)),
        "log_norm": jnp.clip(2.0 + 2.0 * jax.random.uniform(seeds[4], (SEQ, Q_HEADS), jnp.float32) ** block_scale(seeds[4], (SEQ, Q_HEADS), ((0, 32),), -0.2, 0.2), 2.0, 4.0),
        "row_delta": scatter_about(seeds[5], (SEQ, Q_HEADS), 2.0, 10.0, ((0, 32),), jnp.float32),
        "tile_pairs": draw_tile_pairs(jax.random.fold_in(seeds[8], 71), 0),
        "pair_count": draw_pair_count(jax.random.fold_in(seeds[8], 71), 0),
    }


def tile_terms(query_tile, grad_tile, norm_tile, delta_tile, key_tile, value_tile, allowed, scaling):
    scores = jnp.einsum("ikgd,jkd->kgij", query_tile, key_tile) * scaling
    probs = jnp.where(allowed, jnp.exp(scores - norm_tile), 0.0)
    prob_grad = jnp.einsum("ikgd,jkd->kgij", grad_tile, value_tile)
    score_low = (scaling * probs * (prob_grad - delta_tile)).astype(jnp.bfloat16)
    score_grad = lax.optimization_barrier(score_low).astype(jnp.float32)
    probs_low = lax.optimization_barrier(probs.astype(jnp.bfloat16)).astype(jnp.float32)
    query_term = jnp.einsum("kgij,jkd->ikgd", score_grad, key_tile)
    key_term = jnp.einsum("kgij,ikgd->jkd", score_grad, query_tile)
    value_term = jnp.einsum("kgij,ikgd->jkd", probs_low, grad_tile)
    return query_term, key_term, value_term


def add_rows(total, term, start):
    current = lax.dynamic_slice_in_dim(total, start, term.shape[0], 0)
    return lax.dynamic_update_slice_in_dim(total, current + term, start, 0)


def reference(queries, keys, values, out_grad, log_norm, row_delta, tile_pairs, pair_count):
    scaling = HEAD_DIM ** -0.5
    group_size = Q_HEADS // KV_HEADS
    query_blocks = queries.reshape(N_CTX, BLOCK, KV_HEADS, group_size, HEAD_DIM)
    grad_blocks = out_grad.reshape(N_CTX, BLOCK, KV_HEADS, group_size, HEAD_DIM)
    key_blocks = keys.reshape(N_CTX, BLOCK, KV_HEADS, HEAD_DIM)
    value_blocks = values.reshape(N_CTX, BLOCK, KV_HEADS, HEAD_DIM)
    norm_blocks = log_norm.reshape(N_CTX, BLOCK, KV_HEADS, group_size)
    delta_blocks = row_delta.reshape(N_CTX, BLOCK, KV_HEADS, group_size)
    positions = jnp.arange(TILE, dtype=jnp.int32)
    lower_tri = positions[None, :] <= positions[:, None]

    def one_block(carry, index):
        key_total, value_total = carry
        query_rows = query_blocks[index].astype(jnp.float32)
        grad_rows = grad_blocks[index].astype(jnp.float32)
        norm_cols = jnp.transpose(norm_blocks[index], (1, 2, 0))[..., None]
        delta_cols = jnp.transpose(delta_blocks[index], (1, 2, 0))[..., None]
        query_total = jnp.zeros((BLOCK, KV_HEADS, group_size, HEAD_DIM), jnp.float32)
        for cycle_step in range(WIN):
            source = ((index - cycle_step) % N_CTX).astype(jnp.int32)
            key_rows = key_blocks[source].astype(jnp.float32)
            value_rows = value_blocks[source].astype(jnp.float32)
            pair_list = tile_pairs[index, cycle_step]
            live_count = pair_count[index, cycle_step]
            causal = cycle_step == 0

            def slot_body(slot, state):
                q_total, k_total, v_total = state
                q_start = (pair_list[slot, 0] * TILE).astype(jnp.int32)
                k_start = (pair_list[slot, 1] * TILE).astype(jnp.int32)
                if causal:
                    allowed = (q_start != k_start) | lower_tri
                else:
                    allowed = jnp.ones((TILE, TILE), bool)
                query_term, key_term, value_term = tile_terms(
                    lax.dynamic_slice_in_dim(query_rows, q_start, TILE, 0),
                    lax.dynamic_slice_in_dim(grad_rows, q_start, TILE, 0),
                    lax.dynamic_slice_in_dim(norm_cols, q_start, TILE, 2),
                    lax.dynamic_slice_in_dim(delta_cols, q_start, TILE, 2),
                    lax.dynamic_slice_in_dim(key_rows, k_start, TILE, 0),
                    lax.dynamic_slice_in_dim(value_rows, k_start, TILE, 0),
                    allowed, scaling)
                global_row = (source * BLOCK + k_start).astype(jnp.int32)
                return (add_rows(q_total, query_term, q_start), add_rows(k_total, key_term, global_row), add_rows(v_total, value_term, global_row))

            query_total, key_total, value_total = lax.fori_loop(jnp.int32(0), live_count.astype(jnp.int32), slot_body, (query_total, key_total, value_total))
        return (key_total, value_total), query_total.reshape(BLOCK, Q_HEADS * HEAD_DIM).astype(jnp.bfloat16)

    start_total = jnp.zeros((SEQ, KV_HEADS, HEAD_DIM), jnp.float32)
    (key_total, value_total), query_parts = lax.scan(one_block, (start_total, start_total), jnp.arange(N_CTX, dtype=jnp.int32))
    query_grad = query_parts.reshape(SEQ, Q_HEADS * HEAD_DIM)
    key_grad = key_total.reshape(SEQ, KV_HEADS * HEAD_DIM).astype(jnp.bfloat16)
    value_grad = value_total.reshape(SEQ, KV_HEADS * HEAD_DIM).astype(jnp.bfloat16)
    return (query_grad, key_grad, value_grad)
```

```python
import functools

import jax
import jax.numpy as jnp
from jax import lax
from jax.experimental import pallas as pl
from jax.experimental.pallas import tpu as pltpu
from jax.sharding import PartitionSpec as P

HEAD_DIM = 128
TILE = 128
WIN = 4
LOG2E = 1.4426950408889634
FAR = 1e30
NT = (((1,), (1,)), ((), ()))
NN = (((1,), (0,)), ((), ()))


def dot(a, b, dims):
    return lax.dot_general(a, b, dims, preferred_element_type=jnp.float32)


def swap(value, axis):
    return lax.ppermute(value, axis, [(i, i ^ 1) for i in range(lax.axis_size(axis))])


def routed(value, route, backwards=False):
    count = lax.axis_size("ctx")
    pairs = [(c, route(c)) for c in range(count) if route(c) < count]
    if backwards:
        pairs = [(b, a) for a, b in pairs]
    return lax.ppermute(value, "ctx", pairs)


def two_on(c):
    return c + 2


def one_or_three_on(c):
    return c + 1 if c % 2 == 0 else c + 3


def kernel(tiles, group, slots, split, *refs):
    place, pairs, counts = refs[:3]
    refs = refs[3:]
    if split:
        q_mine, q_far, g_mine, g_far, k_mine, v_mine, kv_far = refs[:7]
        refs = refs[7:]
        q_tile = lambda t: (q_mine if t == 0 else q_far)
        g_tile = lambda t: (g_mine if t == 0 else g_far)
    else:
        q_all, g_all, kv_own = refs[:3]
        refs = refs[3:]
        q_tile = lambda t: q_all.at[t]
        g_tile = lambda t: g_all.at[t]
    rows_ref, kv_two, kv_core, kv_odd = refs[:4]
    refs = refs[4:]
    dq_refs = refs[:2] if split else refs[:1]
    refs = refs[len(dq_refs) :]
    d_own, d_two, d_core, d_odd, live, k_rows, v_rows, k_cols, dk_sum, dv_sum = refs
    scale = HEAD_DIM**-0.5
    odd = place[1]
    step_of = (0, 2, 1 + 2 * odd, 3 - 2 * odd)
    block = tiles * TILE
    chunk = 2 * TILE
    chunks = WIN * block // chunk

    def clear(i, _):
        live[i] = 0
        return _

    lax.fori_loop(0, WIN * tiles * tiles, clear, 0)
    for b in range(WIN):
        step = step_of[b]

        def mark(slot, _, b=b, step=step):
            at = (step * slots + slot) * 2
            q_at, k_at = pairs[at], pairs[at + 1]
            if split:
                q_at, k_at = (q_at + place[0]) % 2, (k_at + place[0]) % 2
            live[(b * tiles + k_at) * tiles + q_at] = 1
            return _

        lax.fori_loop(0, counts[step], mark, 0)

    for b, ref in enumerate((None, kv_two, kv_core, kv_odd)):
        for t in range(tiles):
            at = pl.ds(b * block + t * TILE, TILE)
            if b == 0 and split:
                k, v = (k_mine[...], v_mine[...]) if t == 0 else (kv_far[0], kv_far[1])
            else:
                source = kv_own if b == 0 else ref
                k, v = source[t, 0], source[t, 1]
            k_rows[at, :] = k
            v_rows[at, :] = v
            k_cols[:, at] = k.T
    below = lax.broadcasted_iota(jnp.int32, (TILE, 2 * TILE), 0)
    across = lax.broadcasted_iota(jnp.int32, (TILE, 2 * TILE), 1) % TILE
    causal = below <= across

    for t in range(tiles):
        for pair in range(group // 2):
            first = t == 0 and pair == 0
            cut = pl.ds(pair * 2 * HEAD_DIM, HEAD_DIM), pl.ds((pair * 2 + 1) * HEAD_DIM, HEAD_DIM)
            q_two = jnp.concatenate([q_tile(t)[:, cut[0]], q_tile(t)[:, cut[1]]], axis=0)
            g_two = jnp.concatenate([g_tile(t)[:, cut[0]], g_tile(t)[:, cut[1]]], axis=0)
            norm = [rows_ref[t, 0, 0, pl.ds(pair * 2 + i, 1), :] for i in range(2)]
            delta = [rows_ref[t, 1, 0, pl.ds(pair * 2 + i, 1), :] for i in range(2)]
            norm = jnp.concatenate(norm, axis=1) * LOG2E
            delta = jnp.concatenate(delta, axis=1)

            def one_chunk(n, dq, t=t, first=first, q_two=q_two, g_two=g_two, norm=norm, delta=delta):
                at = pl.ds(n * chunk if isinstance(n, int) else pl.multiple_of(n * chunk, chunk), chunk)
                scores = dot(k_rows[at, :], q_two, NT) * (scale * LOG2E)
                prob_grad = dot(v_rows[at, :], g_two, NT)
                probs, grads = [], []
                for half in range(2):
                    k_at = n * 2 + half
                    part = slice(half * TILE, (half + 1) * TILE)
                    shift = jnp.where(live[k_at * tiles + t] > 0, norm, FAR)
                    power = scores[part] - shift
                    if not isinstance(n, int):
                        power = jnp.where(causal | (k_at != t), power, -FAR)
                    elif k_at == t:
                        power = jnp.where(causal, power, -FAR)
                    prob = jnp.exp2(power)
                    probs.append(prob.astype(jnp.bfloat16))
                    grads.append((prob * (prob_grad[part] - delta)).astype(jnp.bfloat16))
                probs = jnp.concatenate(probs, axis=0)
                grads = jnp.concatenate(grads, axis=0)
                dv = dot(probs, g_two, NN)
                dk = dot(grads, q_two, NN)
                if first:
                    dv_sum[at, :] = dv
                    dk_sum[at, :] = dk
                else:
                    dv_sum[at, :] += dv
                    dk_sum[at, :] += dk
                return dq + dot(k_cols[:, at], grads, NN)

            dq = jnp.zeros((HEAD_DIM, 2 * TILE), jnp.float32)
            if chunks <= 4:
                for n in range(chunks):
                    dq = one_chunk(n, dq)
            else:
                dq = lax.fori_loop(0, chunks, one_chunk, dq)
            dq = ((dq * scale).T).astype(jnp.bfloat16)
            out = dq_refs[t] if split else dq_refs[0].at[t]
            out[:, cut[0]] = dq[:TILE]
            out[:, cut[1]] = dq[TILE:]

    for b, ref in enumerate((d_own, d_two, d_core, d_odd)):
        for t in range(tiles):
            at = pl.ds(b * block + t * TILE, TILE)
            ref[t, 0] = (dk_sum[at, :] * scale).astype(ref.dtype)
            ref[t, 1] = dv_sum[at, :].astype(ref.dtype)


def per_device(queries, keys, values, out_grad, log_norm, row_delta, tile_pairs, pair_count):
    heads = lax.axis_size("head")
    mine = lax.axis_index("head")
    odd = lax.axis_index("ctx") % 2
    rows = queries.shape[0]
    width = queries.shape[1] // heads
    kv_width = keys.shape[1] // heads
    local_kv = kv_width // HEAD_DIM
    group = width // kv_width
    tiles = heads * rows // TILE
    slots = tile_pairs.shape[2]
    split = heads == 2 and rows == TILE
    small = jnp.stack([log_norm.T, row_delta.T])
    small = small.reshape(2, heads, local_kv, group, rows)

    if split:
        def other(x):
            return lax.dynamic_slice_in_dim(x, (1 - mine) * (x.shape[1] // 2), x.shape[1] // 2, 1)

        kv_mine = jnp.stack(
            [
                lax.dynamic_slice_in_dim(x, mine * kv_width, kv_width, 1)
                for x in (keys, values)
            ]
        )
        kv_far = swap(jnp.stack([other(keys), other(values)]), "head")
        kv_own = jnp.stack([kv_mine, kv_far])
        qg_far = swap(jnp.stack([other(queries), other(out_grad)]), "head")
        small_mine = lax.dynamic_index_in_dim(small, mine, 1, keepdims=False)
        small_far = swap(lax.dynamic_index_in_dim(small, 1 - mine, 1, keepdims=False), "head")
        small_all = jnp.stack([small_mine, small_far])
    else:
        def spread(x, split_at):
            got = lax.all_to_all(x, "head", split_axis=split_at, concat_axis=0)
            return got

        kv = jnp.stack([keys, values]).reshape(2, rows, heads, kv_width)
        kv_own = spread(kv, 2)
        q_all = spread(queries.reshape(rows, heads, width), 1)
        g_all = spread(out_grad.reshape(rows, heads, width), 1)
        small_all = spread(small, 1)
        per = rows // TILE
        kv_own = jnp.swapaxes(kv_own.reshape(heads, 2, per, TILE, kv_width), 1, 2)
        kv_own = kv_own.reshape(tiles, 2, TILE, kv_width)
        q_all = q_all.reshape(tiles, TILE, width)
        g_all = g_all.reshape(tiles, TILE, width)
        small_all = small_all.reshape(heads, 2, local_kv, group, per, TILE)
        small_all = jnp.moveaxis(small_all, 4, 1).reshape(tiles, 2, local_kv, group, TILE)

    kv_two = routed(kv_own, two_on)
    kv_odd = routed(kv_own, one_or_three_on)
    kv_core = swap(kv_two, "ctx")

    place = jnp.stack([mine, odd]).astype(jnp.int32)
    kv_spec = pl.BlockSpec((tiles, 2, TILE, HEAD_DIM), lambda h, *_: (0, 0, 0, h))
    wide = group * HEAD_DIM
    if split:
        head_args = (queries, qg_far, out_grad, qg_far, keys, values, kv_far)
        q_own = pl.BlockSpec((rows, wide), lambda h, place, *_: (0, place[0] * local_kv + h))
        k_own = pl.BlockSpec((rows, HEAD_DIM), lambda h, place, *_: (0, place[0] * local_kv + h))
        head_specs = [
            q_own,
            pl.BlockSpec((None, rows, wide), lambda h, *_: (0, 0, h)),
            q_own,
            pl.BlockSpec((None, rows, wide), lambda h, *_: (1, 0, h)),
            k_own,
            k_own,
            pl.BlockSpec((2, rows, HEAD_DIM), lambda h, *_: (0, 0, h)),
        ]
        dq_shapes = [jax.ShapeDtypeStruct((rows, width), jnp.bfloat16)] * 2
        dq_specs = [pl.BlockSpec((rows, wide), lambda h, *_: (0, h))] * 2
    else:
        head_args = (q_all, g_all, kv_own)
        all_spec = pl.BlockSpec((tiles, TILE, wide), lambda h, *_: (0, 0, h))
        head_specs = [all_spec, all_spec, kv_spec]
        dq_shapes = [jax.ShapeDtypeStruct((tiles, TILE, width), jnp.bfloat16)]
        dq_specs = [all_spec]
    small_spec = pl.BlockSpec((tiles, 2, 1, group, TILE), lambda h, *_: (0, 0, h, 0, 0))
    d_shape = (tiles, 2, TILE, kv_width)
    keys_all = WIN * tiles * TILE
    results = pl.pallas_call(
        functools.partial(kernel, tiles, group, slots, split),
        out_shape=dq_shapes
        + [jax.ShapeDtypeStruct(d_shape, t) for t in (jnp.float32, jnp.float32, jnp.bfloat16, jnp.bfloat16)],
        grid_spec=pltpu.PrefetchScalarGridSpec(
            num_scalar_prefetch=3,
            grid=(local_kv,),
            in_specs=head_specs + [small_spec, kv_spec, kv_spec, kv_spec],
            out_specs=dq_specs + [kv_spec] * 4,
            scratch_shapes=[
                pltpu.SMEM((WIN * tiles * tiles,), jnp.int32),
                pltpu.VMEM((keys_all, HEAD_DIM), jnp.bfloat16),
                pltpu.VMEM((keys_all, HEAD_DIM), jnp.bfloat16),
                pltpu.VMEM((HEAD_DIM, keys_all), jnp.bfloat16),
                pltpu.VMEM((keys_all, HEAD_DIM), jnp.float32),
                pltpu.VMEM((keys_all, HEAD_DIM), jnp.float32),
            ],
        ),
        compiler_params=pltpu.CompilerParams(vmem_limit_bytes=48 * 1024 * 1024),
        name="attention_grads",
    )(
        place,
        tile_pairs.reshape(-1),
        pair_count.reshape(-1),
        *head_args,
        small_all,
        kv_two,
        kv_core,
        kv_odd,
    )
    d_own, d_two, d_core, d_odd = results[-4:]
    from_odd = routed(d_odd, one_or_three_on, backwards=True)
    d_two = d_two + swap(d_core, "ctx").astype(jnp.float32)
    from_two = routed(d_two.astype(jnp.bfloat16), two_on, backwards=True)
    d_all = (d_own + from_odd.astype(jnp.float32) + from_two.astype(jnp.float32)).astype(jnp.bfloat16)

    if split:
        dq_mine, dq_other = results[:2]
        dq_far = swap(dq_other, "head")
        d_far = swap(d_all[1], "head")

        def whole(near, far):
            return jnp.where(
                mine == 0, jnp.concatenate([near, far], -1), jnp.concatenate([far, near], -1)
            )

        d_both = whole(d_all[0], d_far)
        return whole(dq_mine, dq_far), d_both[0], d_both[1]
    dq = results[0].reshape(heads, rows, width)
    dq = lax.all_to_all(dq, "head", split_axis=0, concat_axis=1).reshape(queries.shape)
    d_all = jnp.swapaxes(d_all.reshape(heads, rows // TILE, 2, TILE, kv_width), 1, 2)
    d_all = d_all.reshape(heads, 2, rows, kv_width)
    d_all = lax.all_to_all(d_all, "head", split_axis=0, concat_axis=2).reshape(2, *keys.shape)
    return dq, d_all[0], d_all[1]


def solution(mesh):
    rows = P(("ctx", "head"), None)
    return jax.shard_map(
        per_device,
        mesh=mesh,
        in_specs=(rows,) * 6 + (P("ctx", None, None, None), P("ctx", None)),
        out_specs=(rows,) * 3,
        check_vma=False,
    )
```

```python
import functools

import jax
import jax.numpy as jnp
from jax import lax
from jax.experimental import pallas as pl
from jax.experimental.pallas import tpu as pltpu
from jax.sharding import PartitionSpec as P

HEAD_DIM = 128
TILE = 128
WIN = 4
LOG2E = 1.4426950408889634
FAR = 1e30
PARTS = 2
TOUCH_COST = 6000000000
VMEM_LIMIT = 60 * 1024 * 1024
FIRST_COST, SECOND_COST, DQ_COST, PACK_COST = 1000, 1000, 15000000000, 1000
NT = (((1,), (1,)), ((), ()))
NN = (((1,), (0,)), ((), ()))


def dot(a, b, dims):
    return lax.dot_general(a, b, dims, preferred_element_type=jnp.float32)


def swap(value, axis):
    return lax.ppermute(value, axis, [(i, i ^ 1) for i in range(lax.axis_size(axis))])


def routed(value, route, backwards=False):
    count = lax.axis_size("ctx")
    pairs = [(c, route(c)) for c in range(count) if route(c) < count]
    if backwards:
        pairs = [(b, a) for a, b in pairs]
    return lax.ppermute(value, "ctx", pairs)


def two_on(c):
    return c + 2


def one_or_three_on(c):
    return c + 1 if c % 2 == 0 else c + 3


def mark_live(tiles, slots, turn, steps, pairs, counts, live):
    def clear(i, _):
        live[i] = 0
        return _

    lax.fori_loop(0, WIN * tiles * tiles, clear, 0)
    for b, step in steps:

        def mark(slot, _, b=b, step=step):
            q_at, k_at = pairs[0, step, 0, slot], pairs[0, step, 1, slot]
            if tiles == 2:
                q_at, k_at = (q_at + turn) % 2, (k_at + turn) % 2
            live[(b * tiles + k_at) * tiles + q_at] = 1
            return _

        lax.fori_loop(0, counts[0, step], mark, 0)


def block_kernel(tiles, group, slots, *refs):
    pairs, counts, q_all, g_all, rows_ref, kv_own, kv_two, kv_core, kv_odd = refs[:9]
    dq_ref, d_own, d_two, d_core, d_odd, live, k_rows, v_rows, k_cols, dk_sum, dv_sum = refs[9:]
    scale = HEAD_DIM**-0.5
    odd = lax.axis_index("ctx") % 2
    block = tiles * TILE
    chunk = 2 * TILE
    steps = enumerate((0, 2, 1 + 2 * odd, 3 - 2 * odd))
    mark_live(tiles, slots, 0, steps, pairs, counts, live)
    for b, ref in enumerate((kv_own, kv_two, kv_core, kv_odd)):
        for t in range(tiles):
            at = pl.ds(b * block + t * TILE, TILE)
            k_rows[at, :] = ref[t, 0]
            v_rows[at, :] = ref[t, 1]
            k_cols[:, at] = ref[t, 0].T
    below = lax.broadcasted_iota(jnp.int32, (TILE, 2 * TILE), 0)
    across = lax.broadcasted_iota(jnp.int32, (TILE, 2 * TILE), 1) % TILE
    causal = below <= across

    for t in range(tiles):
        for pair in range(group // 2):
            first = t == 0 and pair == 0
            cut = pl.ds(pair * 2 * HEAD_DIM, HEAD_DIM), pl.ds((pair * 2 + 1) * HEAD_DIM, HEAD_DIM)
            q_two = jnp.concatenate([q_all[t, :, cut[0]], q_all[t, :, cut[1]]], axis=0)
            g_two = jnp.concatenate([g_all[t, :, cut[0]], g_all[t, :, cut[1]]], axis=0)
            norm = [rows_ref[t, 0, 0, pl.ds(pair * 2 + i, 1), :] for i in range(2)]
            delta = [rows_ref[t, 1, 0, pl.ds(pair * 2 + i, 1), :] for i in range(2)]
            norm = jnp.concatenate(norm, axis=1) * LOG2E
            delta = jnp.concatenate(delta, axis=1)

            def one_chunk(n, dq, t=t, first=first, q_two=q_two, g_two=g_two, norm=norm, delta=delta):
                at = pl.ds(pl.multiple_of(n * chunk, chunk), chunk)
                scores = dot(k_rows[at, :], q_two, NT) * (scale * LOG2E)
                prob_grad = dot(v_rows[at, :], g_two, NT)
                probs, grads = [], []
                for half in range(2):
                    k_at = n * 2 + half
                    part = slice(half * TILE, (half + 1) * TILE)
                    shift = jnp.where(live[k_at * tiles + t] > 0, norm, FAR)
                    power = jnp.where(causal | (k_at != t), scores[part] - shift, -FAR)
                    prob = jnp.exp2(power)
                    probs.append(prob.astype(jnp.bfloat16))
                    grads.append((prob * (prob_grad[part] - delta)).astype(jnp.bfloat16))
                probs = jnp.concatenate(probs, axis=0)
                grads = jnp.concatenate(grads, axis=0)
                dv = dot(probs, g_two, NN)
                dk = dot(grads, q_two, NN)
                if first:
                    dv_sum[at, :] = dv
                    dk_sum[at, :] = dk
                else:
                    dv_sum[at, :] += dv
                    dk_sum[at, :] += dk
                return dq + dot(k_cols[:, at], grads, NN)

            dq = jnp.zeros((HEAD_DIM, 2 * TILE), jnp.float32)
            dq = lax.fori_loop(0, WIN * block // chunk, one_chunk, dq)
            dq = ((dq * scale).T).astype(jnp.bfloat16)
            dq_ref[t, :, cut[0]] = dq[:TILE]
            dq_ref[t, :, cut[1]] = dq[TILE:]

    for b, ref in enumerate((d_own, d_two, d_core, d_odd)):
        for t in range(tiles):
            at = pl.ds(b * block + t * TILE, TILE)
            ref[t, 0] = (dk_sum[at, :] * scale).astype(ref.dtype)
            ref[t, 1] = dv_sum[at, :].astype(ref.dtype)


def pair_kernel(group, slots, blocks, n_unused, *refs):
    refs = list(refs)
    mine, pairs, counts, q_mine, q_far, g_mine, g_far, rows_mine, rows_far = refs[:9]
    del refs[:9]
    sources = {}
    for b in blocks:
        sources[b] = tuple(refs[: 3 if b == 0 else 2])
        del refs[: len(sources[b])]
    del refs[:n_unused]
    dq_outs = (refs.pop(0), refs.pop(0))
    outs = {b: (refs.pop(0), refs.pop(0)) for b in blocks}
    live, k_cols, prob_all, grad_all = refs[-4:]
    scale = HEAD_DIM**-0.5
    odd = lax.axis_index("ctx") % 2
    block = 2 * TILE
    units = [(t, pair) for t in range(2) for pair in range(group // 2)]
    step_of = (0, 2, 1 + 2 * odd, 3 - 2 * odd)
    mark_live(2, slots, mine[0], [(b, step_of[b]) for b in blocks], pairs, counts, live)

    below = lax.broadcasted_iota(jnp.int32, (TILE, 2 * TILE), 0)
    across = lax.broadcasted_iota(jnp.int32, (TILE, 2 * TILE), 1) % TILE
    causal = below <= across
    sides = ((q_mine, g_mine), (q_far, g_far))

    def heads_of(ref):
        return [ref[:, i * HEAD_DIM : (i + 1) * HEAD_DIM] for i in range(group)]

    q_all = jnp.concatenate([x for q, g in sides for x in heads_of(q)], axis=0)
    g_all = jnp.concatenate([x for q, g in sides for x in heads_of(g)], axis=0)
    far = rows_far[...].astype(jnp.float32)
    far = far[:, 0:1] + far[:, 1:2] + far[:, 2:3]
    rows = []
    for t, pair in units:
        at = slice(pair * block, (pair + 1) * block)
        norm, delta = [(rows_mine[i, :, at], far[i, :, at])[t] for i in range(2)]
        rows.append((norm * LOG2E, delta))

    for n, b in enumerate(blocks):
        if b == 0:
            k_mine, v_mine, kv_far = sources[b]
            k = jnp.concatenate([k_mine[...], kv_far[0]], axis=0)
            v = jnp.concatenate([v_mine[...], kv_far[1]], axis=0)
        else:
            kv_near, kv_far = sources[b]
            k = jnp.concatenate([kv_near[0], kv_far[0]], axis=0)
            v = jnp.concatenate([kv_near[1], kv_far[1]], axis=0)
        at = slice(n * block, (n + 1) * block)
        k_cols[:, at] = k.T
        for u, (t, pair) in enumerate(units):
            cut = slice(u * block, (u + 1) * block)
            norm, delta = rows[u]
            scores = dot(k, q_all[cut], NT) * (scale * LOG2E)
            prob_grad = dot(v, g_all[cut], NT)
            for k_at in range(2):
                part = slice(k_at * TILE, (k_at + 1) * TILE)
                shift = jnp.where(live[(b * 2 + k_at) * 2 + t] > 0, norm, FAR)
                power = scores[part] - shift
                if b == 0 and k_at == t:
                    power = jnp.where(causal, power, -FAR)
                prob = jnp.exp2(power)
                to = slice(n * block + k_at * TILE, n * block + (k_at + 1) * TILE)
                prob_all[to, cut] = prob.astype(jnp.bfloat16)
                grad_all[to, cut] = (prob * (prob_grad[part] - delta)).astype(jnp.bfloat16)
        dv = dot(prob_all[at, :], g_all, NN)
        dk = dot(grad_all[at, :], q_all, NN) * scale
        for t, out in enumerate(outs[b]):
            part = slice(t * TILE, (t + 1) * TILE)
            out[0] = dk[part].astype(out.dtype)
            out[1] = dv[part].astype(out.dtype)

    for u, (t, pair) in enumerate(units):
        cut = slice(u * block, (u + 1) * block)
        dq = dot(k_cols[...], grad_all[:, cut], NN)
        dq = (dq * scale).T.astype(jnp.bfloat16)
        for i in range(2):
            head = pair * 2 + i
            dq_outs[t][:, head * HEAD_DIM : (head + 1) * HEAD_DIM] = dq[i * TILE : (i + 1) * TILE]


def by_blocks(queries, keys, values, out_grad, log_norm, row_delta, tile_pairs, pair_count):
    heads = lax.axis_size("head")
    rows = queries.shape[0]
    width = queries.shape[1] // heads
    kv_width = keys.shape[1] // heads
    local_kv = kv_width // HEAD_DIM
    group = width // kv_width
    tiles = heads * rows // TILE
    per = rows // TILE

    def spread(x, split_at):
        return lax.all_to_all(x, "head", split_axis=split_at, concat_axis=0)

    kv_own = spread(jnp.stack([keys, values]).reshape(2, rows, heads, kv_width), 2)
    kv_own = jnp.swapaxes(kv_own.reshape(heads, 2, per, TILE, kv_width), 1, 2)
    kv_own = kv_own.reshape(tiles, 2, TILE, kv_width)
    q_all = spread(queries.reshape(rows, heads, width), 1).reshape(tiles, TILE, width)
    g_all = spread(out_grad.reshape(rows, heads, width), 1).reshape(tiles, TILE, width)
    small = jnp.stack([log_norm.T, row_delta.T]).reshape(2, heads, local_kv, group, rows)
    small = spread(small, 1).reshape(heads, 2, local_kv, group, per, TILE)
    small = jnp.moveaxis(small, 4, 1).reshape(tiles, 2, local_kv, group, TILE)

    kv_two = routed(kv_own, two_on)
    kv_odd = routed(kv_own, one_or_three_on)
    kv_core = swap(kv_two, "ctx")

    kv_spec = pl.BlockSpec((tiles, 2, TILE, HEAD_DIM), lambda h, *_: (0, 0, 0, h))
    q_spec = pl.BlockSpec((tiles, TILE, group * HEAD_DIM), lambda h, *_: (0, 0, h))
    small_spec = pl.BlockSpec((tiles, 2, 1, group, TILE), lambda h, *_: (0, 0, h, 0, 0))
    keys_all = WIN * tiles * TILE
    kinds = (jnp.float32, jnp.float32, jnp.bfloat16, jnp.bfloat16)
    dq, d_own, d_two, d_core, d_odd = pl.pallas_call(
        functools.partial(block_kernel, tiles, group, tile_pairs.shape[2]),
        out_shape=[jax.ShapeDtypeStruct(q_all.shape, jnp.bfloat16)]
        + [jax.ShapeDtypeStruct(kv_own.shape, t) for t in kinds],
        grid_spec=pltpu.PrefetchScalarGridSpec(
            num_scalar_prefetch=2,
            grid=(local_kv,),
            in_specs=[q_spec, q_spec, small_spec] + [kv_spec] * 4,
            out_specs=[q_spec] + [kv_spec] * 4,
            scratch_shapes=[
                pltpu.SMEM((WIN * tiles * tiles,), jnp.int32),
                pltpu.VMEM((keys_all, HEAD_DIM), jnp.bfloat16),
                pltpu.VMEM((keys_all, HEAD_DIM), jnp.bfloat16),
                pltpu.VMEM((HEAD_DIM, keys_all), jnp.bfloat16),
                pltpu.VMEM((keys_all, HEAD_DIM), jnp.float32),
                pltpu.VMEM((keys_all, HEAD_DIM), jnp.float32),
            ],
        ),
        compiler_params=pltpu.CompilerParams(vmem_limit_bytes=48 * 1024 * 1024),
        name="block_grads",
    )(jnp.swapaxes(tile_pairs, 2, 3), pair_count, q_all, g_all, small, kv_own, kv_two, kv_core, kv_odd)
    d_all = home(d_own, d_two, d_core, d_odd)
    dq = lax.all_to_all(dq.reshape(heads, rows, width), "head", split_axis=0, concat_axis=1)
    d_all = jnp.swapaxes(d_all.reshape(heads, per, 2, TILE, kv_width), 1, 2)
    d_all = d_all.reshape(heads, 2, rows, kv_width)
    d_all = lax.all_to_all(d_all, "head", split_axis=0, concat_axis=2).reshape(2, *keys.shape)
    return dq.reshape(queries.shape), d_all[0], d_all[1]


def home(d_own, d_two, d_core, d_odd):
    from_odd = routed(d_odd, one_or_three_on, backwards=True)
    d_two = d_two + swap(d_core, "ctx").astype(jnp.float32)
    from_two = routed(d_two.astype(jnp.bfloat16), two_on, backwards=True)
    total = d_own + from_odd.astype(jnp.float32) + from_two.astype(jnp.float32)
    return total.astype(jnp.bfloat16)


def then(value, *before):
    return lax.optimization_barrier((value, *before))[0]


def pack_kernel(heads, mine, q_far, g_far, norm, delta, *outs):
    *parts, rows = outs
    size = parts[0].shape[2]
    tile = q_far.shape[0]
    for p, part in enumerate(parts):
        cut = slice(p * size, (p + 1) * size)
        part[0, :tile] = q_far[:, cut]
        part[1, :tile] = g_far[:, cut]
    for i, ref in enumerate((norm, delta)):
        both = ref[...]
        low_side = mine[0] == 0
        own = jnp.where(low_side, both[:heads], both[heads:])
        other = jnp.where(low_side, both[heads:], both[:heads])
        high = other.astype(jnp.bfloat16)
        rest = other - high.astype(jnp.float32)
        middle = rest.astype(jnp.bfloat16)
        low = (rest - middle.astype(jnp.float32)).astype(jnp.bfloat16)
        for h in range(heads):
            rows[i, :, h * tile : (h + 1) * tile] = own[h : h + 1]
        pad = jnp.zeros((13, tile), jnp.float32)
        per = size // tile
        for h in range(heads):
            three = [x[h : h + 1].astype(jnp.float32) for x in (high, middle, low)]
            block = jnp.concatenate(three + [pad], axis=0).astype(jnp.bfloat16)
            at = h % per
            parts[h // per][i, tile:, at * tile : (at + 1) * tile] = block


def fill_kernel(mine, got, before, half):
    half[...] = got[...]


def touch_kernel(x_ref, y_ref, mark):
    mark[0] = 1


def touch(x, cost):
    return pl.pallas_call(
        touch_kernel,
        out_shape=jax.ShapeDtypeStruct(x.shape, x.dtype),
        in_specs=[pl.BlockSpec(memory_space=pl.ANY)],
        out_specs=pl.BlockSpec(memory_space=pl.ANY),
        input_output_aliases={0: 0},
        scratch_shapes=[pltpu.SMEM((1,), jnp.int32)],
        cost_estimate=pl.CostEstimate(flops=cost, bytes_accessed=1, transcendentals=0),
        name="arrived",
    )(x)


def by_pairs(queries, keys, values, out_grad, log_norm, row_delta, tile_pairs, pair_count):
    mine = lax.axis_index("head")
    rows = queries.shape[0]
    width = queries.shape[1] // 2
    kv_width = keys.shape[1] // 2
    local_kv = kv_width // HEAD_DIM
    group = width // kv_width
    kvs = local_kv // PARTS
    wide = group * HEAD_DIM
    lists = (mine.reshape(1), jnp.swapaxes(tile_pairs, 2, 3), pair_count)

    def cut(x, side):
        size = x.shape[1] // 2
        return lax.dynamic_slice_in_dim(x, side * size, size, 1)

    kv_near = jnp.stack([cut(keys, mine), cut(values, mine)])
    kv_far = swap(jnp.stack([cut(keys, 1 - mine), cut(values, 1 - mine)]), "head")
    kv_far = touch(kv_far, TOUCH_COST)
    pack_spec = pl.BlockSpec((rows, width), lambda i, mine: (0, 1 - mine[0]))
    whole_spec = pl.BlockSpec((2 * local_kv * group, rows), lambda i, mine: (0, 0))
    packed = [(2, rows + 16, kvs * wide)] * PARTS
    *qg_send, small = pl.pallas_call(
        functools.partial(pack_kernel, local_kv * group),
        out_shape=[jax.ShapeDtypeStruct(s, jnp.bfloat16) for s in packed]
        + [jax.ShapeDtypeStruct((2, 1, width), jnp.float32)],
        grid_spec=pltpu.PrefetchScalarGridSpec(
            num_scalar_prefetch=1,
            grid=(1,),
            in_specs=[pack_spec, pack_spec, whole_spec, whole_spec],
            out_specs=[pl.BlockSpec(s, lambda i, mine: (0, 0, 0)) for s in packed + [(2, 1, width)]],
        ),
        compiler_params=pltpu.CompilerParams(vmem_limit_bytes=VMEM_LIMIT),
        cost_estimate=pl.CostEstimate(flops=PACK_COST, bytes_accessed=1, transcendentals=0),
        name="pack_sends",
    )(lists[0], queries, out_grad, log_norm.T, row_delta.T)
    qg_far = [swap(x, "head") for x in qg_send]
    near_two, near_odd = routed(kv_near, two_on), routed(kv_near, one_or_three_on)
    far_two, far_odd = routed(kv_far, two_on), routed(kv_far, one_or_three_on)
    near_core = swap(near_two, "ctx")

    def attend(part, blocks, sources, before, cost):
        first = part * kvs

        def at_mine(h, mine, *_):
            return (0, mine[0] * local_kv + first + h)

        q_own = pl.BlockSpec((rows, wide), at_mine)
        k_own = pl.BlockSpec((rows, HEAD_DIM), at_mine)
        far = lambda i: pl.BlockSpec((None, rows, wide), lambda h, *_: (i, 0, h))
        kv_spec = pl.BlockSpec((2, rows, HEAD_DIM), lambda h, *_: (0, 0, first + h))
        dq_spec = pl.BlockSpec((rows, wide), lambda h, *_: (0, h))
        carry_spec = pl.BlockSpec((None, HEAD_DIM, 2 * group * TILE), lambda h, *_: (h, 0, 0))
        args = [queries, qg_far[part], out_grad, qg_far[part], small, qg_far[part]]
        specs = [
            q_own,
            far(0),
            q_own,
            far(1),
            pl.BlockSpec((2, 1, wide), lambda h, *_: (0, 0, first + h)),
            pl.BlockSpec((2, 16, wide), lambda h, *_: (0, rows // 16, h)),
        ]
        for b in blocks:
            args += sources[b]
            specs += [k_own, k_own, kv_spec] if b == 0 else [kv_spec, kv_spec]
        dq_shapes = [queries.shape, (rows, width)]
        outs = [jax.ShapeDtypeStruct(s, jnp.bfloat16) for s in dq_shapes]
        out_specs = [q_own, pl.BlockSpec((rows, wide), lambda h, *_: (0, first + h))]
        kinds = (jnp.float32, jnp.float32, jnp.bfloat16, jnp.bfloat16)
        outs += [jax.ShapeDtypeStruct((2, rows, kv_width), kinds[b]) for b in blocks for _ in range(2)]
        out_specs += [kv_spec] * (2 * len(blocks))
        alias, n_args = {}, len(args)
        if before is not None:
            for i, array in enumerate(before):
                alias[len(lists) + len(args)] = i
                args.append(array)
        specs += [pl.BlockSpec(memory_space=pl.ANY)] * (len(args) - n_args)
        keys_all = len(blocks) * 2 * TILE
        return pl.pallas_call(
            functools.partial(
                pair_kernel,
                group,
                tile_pairs.shape[2],
                blocks,
                len(args) - n_args,
            ),
            out_shape=outs,
            grid_spec=pltpu.PrefetchScalarGridSpec(
                num_scalar_prefetch=3,
                grid=(kvs,),
                in_specs=specs,
                out_specs=out_specs,
                scratch_shapes=[
                    pltpu.SMEM((WIN * 4,), jnp.int32),
                    pltpu.VMEM((HEAD_DIM, keys_all), jnp.bfloat16),
                    pltpu.VMEM((keys_all, 2 * group * TILE), jnp.bfloat16),
                    pltpu.VMEM((keys_all, 2 * group * TILE), jnp.bfloat16),
                ],
            ),
            input_output_aliases=alias,
            compiler_params=pltpu.CompilerParams(vmem_limit_bytes=VMEM_LIMIT),
            cost_estimate=pl.CostEstimate(flops=cost, bytes_accessed=1, transcendentals=0),
            name="grads_" + "".join(map(str, blocks)) + "_part" + str(part),
        )(*lists, *args)

    sources = {
        0: (keys, values, kv_far),
        1: (near_two, far_two),
        2: (near_core, swap(far_two, "ctx")),
        3: (near_odd, far_odd),
    }
    done = None
    for part, cost in enumerate((FIRST_COST, SECOND_COST)):
        done = attend(part, (0, 1, 2, 3), sources, done, cost)
    dq_near, dq_far, *sums = done
    own_sums, sums = sums[:2], sums[2:]

    def wide_sum(*terms):
        return sum(x.astype(jnp.float32) for x in terms).astype(jnp.bfloat16)

    totals = []
    for t in (1, 0):
        two = wide_sum(sums[t], swap(sums[2 + t], "ctx"))
        two = routed(two, two_on, backwards=True)
        odd = routed(sums[4 + t], one_or_three_on, backwards=True)
        totals.append(wide_sum(own_sums[t], odd, two))
    far, near = totals

    def whole(near, far):
        return jnp.where(mine == 0, jnp.concatenate(near + far, -1), jnp.concatenate(far + near, -1))

    both = whole([near], [swap(far, "head")])
    half = pl.BlockSpec((rows, width), lambda i, mine: (0, 1 - mine[0]))
    dq = pl.pallas_call(
        fill_kernel,
        out_shape=jax.ShapeDtypeStruct(queries.shape, jnp.bfloat16),
        grid_spec=pltpu.PrefetchScalarGridSpec(
            num_scalar_prefetch=1,
            grid=(1,),
            in_specs=[
                pl.BlockSpec((rows, width), lambda i, mine: (0, 0)),
                pl.BlockSpec(memory_space=pl.ANY),
            ],
            out_specs=half,
        ),
        input_output_aliases={2: 0},
        cost_estimate=pl.CostEstimate(flops=DQ_COST, bytes_accessed=1, transcendentals=0),
        name="fill_in",
    )(lists[0], swap(dq_far, "head"), dq_near)
    return dq, both[0], both[1]


def per_device(queries, keys, values, out_grad, log_norm, row_delta, tile_pairs, pair_count):
    heads = lax.axis_size("head")
    local_kv = keys.shape[1] // heads // HEAD_DIM
    group = queries.shape[1] // keys.shape[1]
    paired = heads == 2 and queries.shape[0] == TILE and local_kv % PARTS == 0 and group % 2 == 0
    form = by_pairs if paired else by_blocks
    return form(queries, keys, values, out_grad, log_norm, row_delta, tile_pairs, pair_count)


def solution(mesh):
    rows = P(("ctx", "head"), None)
    return jax.shard_map(
        per_device,
        mesh=mesh,
        in_specs=(rows,) * 6 + (P("ctx", None, None, None), P("ctx", None)),
        out_specs=(rows,) * 3,
        check_vma=False,
    )
```

```python
import functools

import jax
import jax.numpy as jnp
from jax import lax
from jax.experimental import pallas as pl
from jax.experimental.pallas import tpu as pltpu
from jax.sharding import PartitionSpec as P

HEAD_DIM = 128
TILE = 128
WIN = 4
LOG2E = 1.4426950408889634
FAR = 1e30
PARTS = 2
TOUCH_COST = 6000000000
VMEM_LIMIT = 20 * 1024 * 1024
SMALL_LIMIT = 60 * 1024 * 1024
FIRST_COST, SECOND_COST, DQ_COST, PACK_COST = 3000000000, 10000000000, 1000, 1000
NT = (((1,), (1,)), ((), ()))
NN = (((1,), (0,)), ((), ()))


def dot(a, b, dims):
    return lax.dot_general(a, b, dims, preferred_element_type=jnp.float32)


def swap(value, axis):
    return lax.ppermute(value, axis, [(i, i ^ 1) for i in range(lax.axis_size(axis))])


def routed(value, route, backwards=False):
    count = lax.axis_size("ctx")
    pairs = [(c, route(c)) for c in range(count) if route(c) < count]
    if backwards:
        pairs = [(b, a) for a, b in pairs]
    return lax.ppermute(value, "ctx", pairs)


def two_on(c):
    return c + 2


def one_or_three_on(c):
    return c + 1 if c % 2 == 0 else c + 3


def mark_live(tiles, slots, turn, steps, pairs, counts, live):
    def clear(i, _):
        live[i] = 0
        return _

    lax.fori_loop(0, WIN * tiles * tiles, clear, 0)
    for b, step in steps:

        def mark(slot, _, b=b, step=step):
            q_at, k_at = pairs[0, step, 0, slot], pairs[0, step, 1, slot]
            if tiles == 2:
                q_at, k_at = (q_at + turn) % 2, (k_at + turn) % 2
            live[(b * tiles + k_at) * tiles + q_at] = 1
            return _

        lax.fori_loop(0, counts[0, step], mark, 0)


def block_kernel(tiles, group, slots, *refs):
    pairs, counts, q_all, g_all, rows_ref, kv_own, kv_two, kv_core, kv_odd = refs[:9]
    dq_ref, d_own, d_two, d_core, d_odd, live, k_rows, v_rows, k_cols, dk_sum, dv_sum = refs[9:]
    scale = HEAD_DIM**-0.5
    odd = lax.axis_index("ctx") % 2
    block = tiles * TILE
    chunk = 2 * TILE
    steps = enumerate((0, 2, 1 + 2 * odd, 3 - 2 * odd))
    mark_live(tiles, slots, 0, steps, pairs, counts, live)
    for b, ref in enumerate((kv_own, kv_two, kv_core, kv_odd)):
        for t in range(tiles):
            at = pl.ds(b * block + t * TILE, TILE)
            k_rows[at, :] = ref[t, 0]
            v_rows[at, :] = ref[t, 1]
            k_cols[:, at] = ref[t, 0].T
    below = lax.broadcasted_iota(jnp.int32, (TILE, 2 * TILE), 0)
    across = lax.broadcasted_iota(jnp.int32, (TILE, 2 * TILE), 1) % TILE
    causal = below <= across

    for t in range(tiles):
        for pair in range(group // 2):
            first = t == 0 and pair == 0
            cut = pl.ds(pair * 2 * HEAD_DIM, HEAD_DIM), pl.ds((pair * 2 + 1) * HEAD_DIM, HEAD_DIM)
            q_two = jnp.concatenate([q_all[t, :, cut[0]], q_all[t, :, cut[1]]], axis=0)
            g_two = jnp.concatenate([g_all[t, :, cut[0]], g_all[t, :, cut[1]]], axis=0)
            norm = [rows_ref[t, 0, 0, pl.ds(pair * 2 + i, 1), :] for i in range(2)]
            delta = [rows_ref[t, 1, 0, pl.ds(pair * 2 + i, 1), :] for i in range(2)]
            norm = jnp.concatenate(norm, axis=1) * LOG2E
            delta = jnp.concatenate(delta, axis=1)

            def one_chunk(n, dq, t=t, first=first, q_two=q_two, g_two=g_two, norm=norm, delta=delta):
                at = pl.ds(pl.multiple_of(n * chunk, chunk), chunk)
                scores = dot(k_rows[at, :], q_two, NT) * (scale * LOG2E)
                prob_grad = dot(v_rows[at, :], g_two, NT)
                probs, grads = [], []
                for half in range(2):
                    k_at = n * 2 + half
                    part = slice(half * TILE, (half + 1) * TILE)
                    shift = jnp.where(live[k_at * tiles + t] > 0, norm, FAR)
                    power = jnp.where(causal | (k_at != t), scores[part] - shift, -FAR)
                    prob = jnp.exp2(power)
                    probs.append(prob.astype(jnp.bfloat16))
                    grads.append((prob * (prob_grad[part] - delta)).astype(jnp.bfloat16))
                probs = jnp.concatenate(probs, axis=0)
                grads = jnp.concatenate(grads, axis=0)
                dv = dot(probs, g_two, NN)
                dk = dot(grads, q_two, NN)
                if first:
                    dv_sum[at, :] = dv
                    dk_sum[at, :] = dk
                else:
                    dv_sum[at, :] += dv
                    dk_sum[at, :] += dk
                return dq + dot(k_cols[:, at], grads, NN)

            dq = jnp.zeros((HEAD_DIM, 2 * TILE), jnp.float32)
            dq = lax.fori_loop(0, WIN * block // chunk, one_chunk, dq)
            dq = ((dq * scale).T).astype(jnp.bfloat16)
            dq_ref[t, :, cut[0]] = dq[:TILE]
            dq_ref[t, :, cut[1]] = dq[TILE:]

    for b, ref in enumerate((d_own, d_two, d_core, d_odd)):
        for t in range(tiles):
            at = pl.ds(b * block + t * TILE, TILE)
            ref[t, 0] = (dk_sum[at, :] * scale).astype(ref.dtype)
            ref[t, 1] = dv_sum[at, :].astype(ref.dtype)


def pair_kernel(part, group, slots, blocks, n_unused, *refs):
    refs = list(refs)
    mine, pairs, counts, q_mine, q_far, g_mine, g_far, rows_mine, rows_far = refs[:9]
    del refs[:9]
    sources = {}
    for b in blocks:
        sources[b] = tuple(refs[: 3 if b == 0 else 2])
        del refs[: len(sources[b])]
    del refs[:n_unused]
    dq_outs = (refs.pop(0), refs.pop(0))
    outs = {}
    for b in blocks:
        first = refs.pop(0)
        outs[b] = (first.at[0], first.at[1]) if b >= 2 else (first, refs.pop(0))
    live, k_cols, prob_all, grad_all = refs[-4:]
    scale = HEAD_DIM**-0.5
    odd = lax.axis_index("ctx") % 2
    block = 2 * TILE
    units = [(t, pair) for t in range(2) for pair in range(group // 2)]
    step_of = (0, 2, 1 + 2 * odd, 3 - 2 * odd)
    mark_live(2, slots, mine[0], [(b, step_of[b]) for b in blocks], pairs, counts, live)

    below = lax.broadcasted_iota(jnp.int32, (TILE, 2 * TILE), 0)
    across = lax.broadcasted_iota(jnp.int32, (TILE, 2 * TILE), 1) % TILE
    causal = below <= across
    sides = ((q_mine, g_mine), (q_far, g_far))

    def heads_of(ref):
        return [ref[:, i * HEAD_DIM : (i + 1) * HEAD_DIM] for i in range(group)]

    q_all = jnp.concatenate([x for q, g in sides for x in heads_of(q)], axis=0)
    g_all = jnp.concatenate([x for q, g in sides for x in heads_of(g)], axis=0)
    far = rows_far[...].astype(jnp.float32)
    far = sum(far[:, part * 3 + i : part * 3 + i + 1] for i in range(3))
    rows = []
    for t, pair in units:
        at = slice(pair * block, (pair + 1) * block)
        norm, delta = [(rows_mine[i, :, at], far[i, :, at])[t] for i in range(2)]
        rows.append((norm * LOG2E, delta))

    for n, b in enumerate(blocks):
        if b == 0:
            k_mine, v_mine, kv_far = sources[b]
            k = jnp.concatenate([k_mine[...], kv_far[0]], axis=0)
            v = jnp.concatenate([v_mine[...], kv_far[1]], axis=0)
        else:
            kv_near, kv_far = sources[b]
            k = jnp.concatenate([kv_near[0], kv_far[0]], axis=0)
            v = jnp.concatenate([kv_near[1], kv_far[1]], axis=0)
        at = slice(n * block, (n + 1) * block)
        k_cols[:, at] = k.T
        for u, (t, pair) in enumerate(units):
            cut = slice(u * block, (u + 1) * block)
            norm, delta = rows[u]
            scores = dot(k, q_all[cut], NT) * (scale * LOG2E)
            prob_grad = dot(v, g_all[cut], NT)
            for k_at in range(2):
                part = slice(k_at * TILE, (k_at + 1) * TILE)
                shift = jnp.where(live[(b * 2 + k_at) * 2 + t] > 0, norm, FAR)
                power = scores[part] - shift
                if b == 0 and k_at == t:
                    power = jnp.where(causal, power, -FAR)
                prob = jnp.exp2(power)
                to = slice(n * block + k_at * TILE, n * block + (k_at + 1) * TILE)
                prob_all[to, cut] = prob.astype(jnp.bfloat16)
                grad_all[to, cut] = (prob * (prob_grad[part] - delta)).astype(jnp.bfloat16)
        dv = dot(prob_all[at, :], g_all, NN)
        dk = dot(grad_all[at, :], q_all, NN) * scale
        for t, out in enumerate(outs[b]):
            part = slice(t * TILE, (t + 1) * TILE)
            out[0] = dk[part].astype(out.dtype)
            out[1] = dv[part].astype(out.dtype)

    for u, (t, pair) in enumerate(units):
        cut = slice(u * block, (u + 1) * block)
        dq = dot(k_cols[...], grad_all[:, cut], NN)
        dq = (dq * scale).T.astype(jnp.bfloat16)
        for i in range(2):
            head = pair * 2 + i
            dq_outs[t][:, head * HEAD_DIM : (head + 1) * HEAD_DIM] = dq[i * TILE : (i + 1) * TILE]


def by_blocks(queries, keys, values, out_grad, log_norm, row_delta, tile_pairs, pair_count):
    heads = lax.axis_size("head")
    rows = queries.shape[0]
    width = queries.shape[1] // heads
    kv_width = keys.shape[1] // heads
    local_kv = kv_width // HEAD_DIM
    group = width // kv_width
    tiles = heads * rows // TILE
    per = rows // TILE

    def spread(x, split_at):
        return lax.all_to_all(x, "head", split_axis=split_at, concat_axis=0)

    kv_own = spread(jnp.stack([keys, values]).reshape(2, rows, heads, kv_width), 2)
    kv_own = jnp.swapaxes(kv_own.reshape(heads, 2, per, TILE, kv_width), 1, 2)
    kv_own = kv_own.reshape(tiles, 2, TILE, kv_width)
    q_all = spread(queries.reshape(rows, heads, width), 1).reshape(tiles, TILE, width)
    g_all = spread(out_grad.reshape(rows, heads, width), 1).reshape(tiles, TILE, width)
    small = jnp.stack([log_norm.T, row_delta.T]).reshape(2, heads, local_kv, group, rows)
    small = spread(small, 1).reshape(heads, 2, local_kv, group, per, TILE)
    small = jnp.moveaxis(small, 4, 1).reshape(tiles, 2, local_kv, group, TILE)

    kv_two = routed(kv_own, two_on)
    kv_odd = routed(kv_own, one_or_three_on)
    kv_core = swap(kv_two, "ctx")

    kv_spec = pl.BlockSpec((tiles, 2, TILE, HEAD_DIM), lambda h, *_: (0, 0, 0, h))
    q_spec = pl.BlockSpec((tiles, TILE, group * HEAD_DIM), lambda h, *_: (0, 0, h))
    small_spec = pl.BlockSpec((tiles, 2, 1, group, TILE), lambda h, *_: (0, 0, h, 0, 0))
    keys_all = WIN * tiles * TILE
    kinds = (jnp.float32, jnp.float32, jnp.bfloat16, jnp.bfloat16)
    dq, d_own, d_two, d_core, d_odd = pl.pallas_call(
        functools.partial(block_kernel, tiles, group, tile_pairs.shape[2]),
        out_shape=[jax.ShapeDtypeStruct(q_all.shape, jnp.bfloat16)]
        + [jax.ShapeDtypeStruct(kv_own.shape, t) for t in kinds],
        grid_spec=pltpu.PrefetchScalarGridSpec(
            num_scalar_prefetch=2,
            grid=(local_kv,),
            in_specs=[q_spec, q_spec, small_spec] + [kv_spec] * 4,
            out_specs=[q_spec] + [kv_spec] * 4,
            scratch_shapes=[
                pltpu.SMEM((WIN * tiles * tiles,), jnp.int32),
                pltpu.VMEM((keys_all, HEAD_DIM), jnp.bfloat16),
                pltpu.VMEM((keys_all, HEAD_DIM), jnp.bfloat16),
                pltpu.VMEM((HEAD_DIM, keys_all), jnp.bfloat16),
                pltpu.VMEM((keys_all, HEAD_DIM), jnp.float32),
                pltpu.VMEM((keys_all, HEAD_DIM), jnp.float32),
            ],
        ),
        compiler_params=pltpu.CompilerParams(vmem_limit_bytes=48 * 1024 * 1024),
        name="block_grads",
    )(jnp.swapaxes(tile_pairs, 2, 3), pair_count, q_all, g_all, small, kv_own, kv_two, kv_core, kv_odd)
    d_all = home(d_own, d_two, d_core, d_odd)
    dq = lax.all_to_all(dq.reshape(heads, rows, width), "head", split_axis=0, concat_axis=1)
    d_all = jnp.swapaxes(d_all.reshape(heads, per, 2, TILE, kv_width), 1, 2)
    d_all = d_all.reshape(heads, 2, rows, kv_width)
    d_all = lax.all_to_all(d_all, "head", split_axis=0, concat_axis=2).reshape(2, *keys.shape)
    return dq.reshape(queries.shape), d_all[0], d_all[1]


def home(d_own, d_two, d_core, d_odd):
    from_odd = routed(d_odd, one_or_three_on, backwards=True)
    d_two = d_two + swap(d_core, "ctx").astype(jnp.float32)
    from_two = routed(d_two.astype(jnp.bfloat16), two_on, backwards=True)
    total = d_own + from_odd.astype(jnp.float32) + from_two.astype(jnp.float32)
    return total.astype(jnp.bfloat16)


def then(value, *before):
    return lax.optimization_barrier((value, *before))[0]


def pack_kernel(heads, mine, q_far, g_far, norm, delta, *outs):
    *parts, rows = outs
    size = parts[0].shape[2]
    tile = q_far.shape[0]
    for p, part in enumerate(parts):
        cut = slice(p * size, (p + 1) * size)
        part[0, :tile] = q_far[:, cut]
        part[1, :tile] = g_far[:, cut]
    for i, ref in enumerate((norm, delta)):
        both = ref[...]
        low_side = mine[0] == 0
        own = jnp.where(low_side, both[:heads], both[heads:])
        other = jnp.where(low_side, both[heads:], both[:heads])
        high = other.astype(jnp.bfloat16)
        rest = other - high.astype(jnp.float32)
        middle = rest.astype(jnp.bfloat16)
        low = (rest - middle.astype(jnp.float32)).astype(jnp.bfloat16)
        for h in range(heads):
            rows[i, :, h * tile : (h + 1) * tile] = own[h : h + 1]
        per = size // tile
        pad = [jnp.zeros((16 - 3 * len(parts), tile), jnp.float32)]
        for at in range(per):
            heads_at = [at + p * per for p in range(len(parts))]
            three = [x[h : h + 1].astype(jnp.float32) for h in heads_at for x in (high, middle, low)]
            block = jnp.concatenate(three + pad, axis=0).astype(jnp.bfloat16)
            parts[0][i, tile:, at * tile : (at + 1) * tile] = block


def fill_kernel(mine, first, last, before, half):
    size = first.shape[1]
    half[:, :size] = first[...]
    half[:, size:] = last[...]


def after(value, *before):
    return lax.optimization_barrier((value, *before))[0]


def touch_kernel(x_ref, y_ref, mark):
    mark[0] = 1


def touch(x, cost):
    return pl.pallas_call(
        touch_kernel,
        out_shape=jax.ShapeDtypeStruct(x.shape, x.dtype),
        in_specs=[pl.BlockSpec(memory_space=pl.ANY)],
        out_specs=pl.BlockSpec(memory_space=pl.ANY),
        input_output_aliases={0: 0},
        scratch_shapes=[pltpu.SMEM((1,), jnp.int32)],
        cost_estimate=pl.CostEstimate(flops=cost, bytes_accessed=1, transcendentals=0),
        name="arrived",
    )(x)


def by_pairs(queries, keys, values, out_grad, log_norm, row_delta, tile_pairs, pair_count):
    mine = lax.axis_index("head")
    rows = queries.shape[0]
    width = queries.shape[1] // 2
    kv_width = keys.shape[1] // 2
    local_kv = kv_width // HEAD_DIM
    group = width // kv_width
    kvs = local_kv // PARTS
    wide = group * HEAD_DIM
    lists = (mine.reshape(1), jnp.swapaxes(tile_pairs, 2, 3), pair_count)

    def cut(x, side):
        size = x.shape[1] // 2
        return lax.dynamic_slice_in_dim(x, side * size, size, 1)

    kv_near = jnp.stack([cut(keys, mine), cut(values, mine)])
    kv_far = swap(jnp.stack([cut(keys, 1 - mine), cut(values, 1 - mine)]), "head")
    kv_far = touch(kv_far, TOUCH_COST)
    pack_spec = pl.BlockSpec((rows, width), lambda i, mine: (0, 1 - mine[0]))
    whole_spec = pl.BlockSpec((2 * local_kv * group, rows), lambda i, mine: (0, 0))
    packed = [(2, rows + (16 if part == 0 else 0), kvs * wide) for part in range(PARTS)]
    *qg_send, small = pl.pallas_call(
        functools.partial(pack_kernel, local_kv * group),
        out_shape=[pltpu.HBM(s, jnp.bfloat16) for s in packed]
        + [jax.ShapeDtypeStruct((2, 1, width), jnp.float32)],
        grid_spec=pltpu.PrefetchScalarGridSpec(
            num_scalar_prefetch=1,
            grid=(1,),
            in_specs=[pack_spec, pack_spec, whole_spec, whole_spec],
            out_specs=[pl.BlockSpec(s, lambda i, mine: (0, 0, 0)) for s in packed + [(2, 1, width)]],
        ),
        compiler_params=pltpu.CompilerParams(vmem_limit_bytes=SMALL_LIMIT),
        cost_estimate=pl.CostEstimate(flops=PACK_COST, bytes_accessed=1, transcendentals=0),
        name="pack_sends",
    )(lists[0], queries, out_grad, log_norm.T, row_delta.T)
    qg_far = [swap(x, "head") for x in qg_send]
    near_two, near_odd = routed(kv_near, two_on), routed(after(kv_near, kv_far), one_or_three_on)
    far_two, far_odd = routed(kv_far, two_on), routed(kv_far, one_or_three_on)
    near_core = swap(near_two, "ctx")

    def attend(part, blocks, sources, before, cost):
        first = part * kvs

        def at_mine(h, mine, *_):
            return (0, mine[0] * local_kv + first + h)

        q_own = pl.BlockSpec((rows, wide), at_mine)
        k_own = pl.BlockSpec((rows, HEAD_DIM), at_mine)
        far = lambda i: pl.BlockSpec((None, rows, wide), lambda h, *_: (i, 0, h))
        kv_spec = pl.BlockSpec((2, rows, HEAD_DIM), lambda h, *_: (0, 0, first + h))
        dq_spec = pl.BlockSpec((rows, wide), lambda h, *_: (0, h))
        carry_spec = pl.BlockSpec((None, HEAD_DIM, 2 * group * TILE), lambda h, *_: (h, 0, 0))
        args = [queries, qg_far[part], out_grad, qg_far[part], small, qg_far[0]]
        specs = [
            q_own,
            far(0),
            q_own,
            far(1),
            pl.BlockSpec((2, 1, wide), lambda h, *_: (0, 0, first + h)),
            pl.BlockSpec((2, 16, wide), lambda h, *_: (0, rows // 16, h)),
        ]
        for b in blocks:
            args += sources[b]
            specs += [k_own, k_own, kv_spec] if b == 0 else [kv_spec, kv_spec]
        dq_shapes = [queries.shape, (rows, kvs * wide)]
        outs = [pltpu.HBM(s, jnp.bfloat16) for s in dq_shapes]
        out_specs = [q_own, pl.BlockSpec((rows, wide), lambda h, *_: (0, h))]
        both = lambda width, at: (
            pltpu.HBM((2, 2, rows, width), jnp.bfloat16),
            pl.BlockSpec((2, 2, rows, HEAD_DIM), lambda h, *_: (0, 0, 0, at + h)),
        )
        pairs = [(pltpu.HBM((2, rows, kv_width), jnp.float32), kv_spec)] * 4
        pairs += [both(kv_width, first), both(kvs * HEAD_DIM, 0)]
        for shape, spec in pairs:
            outs.append(shape)
            out_specs.append(spec)
        alias, n_args = {}, len(args)
        if before is not None:
            for i, array in enumerate(before):
                alias[len(lists) + len(args)] = i if i == 0 else i + 1
                args.append(array)
        specs += [pl.BlockSpec(memory_space=pl.ANY)] * (len(args) - n_args)
        keys_all = len(blocks) * 2 * TILE
        return pl.pallas_call(
            functools.partial(
                pair_kernel,
                part,
                group,
                tile_pairs.shape[2],
                blocks,
                len(args) - n_args,
            ),
            out_shape=outs,
            grid_spec=pltpu.PrefetchScalarGridSpec(
                num_scalar_prefetch=3,
                grid=(kvs,),
                in_specs=specs,
                out_specs=out_specs,
                scratch_shapes=[
                    pltpu.SMEM((WIN * 4,), jnp.int32),
                    pltpu.VMEM((HEAD_DIM, keys_all), jnp.bfloat16),
                    pltpu.VMEM((keys_all, 2 * group * TILE), jnp.bfloat16),
                    pltpu.VMEM((keys_all, 2 * group * TILE), jnp.bfloat16),
                ],
            ),
            input_output_aliases=alias,
            compiler_params=pltpu.CompilerParams(vmem_limit_bytes=VMEM_LIMIT),
            cost_estimate=pl.CostEstimate(flops=cost, bytes_accessed=1, transcendentals=0),
            name="grads_" + "".join(map(str, blocks)) + "_part" + str(part),
        )(*lists, *args)

    sources = {
        0: (keys, values, kv_far),
        1: (near_two, far_two),
        2: (near_core, swap(after(far_two, near_odd), "ctx")),
        3: (near_odd, far_odd),
    }
    def wide_sum(*terms):
        return sum(x.astype(jnp.float32) for x in terms).astype(jnp.bfloat16)

    blocks = (0, 1, 2, 3)
    dq_near, dq_far, *sums, odd = attend(0, blocks, sources, None, FIRST_COST)
    dq_first = swap(dq_far, "head")
    odds = [routed(odd, one_or_three_on, backwards=True)]
    results = attend(1, blocks, sources, (dq_near, *sums), SECOND_COST)
    dq_near, dq_far, own_n, own_f, two_n, two_f, core, odd = results
    core = swap(after(core, dq_first, odds[0]), "ctx")
    odds.append(routed(odd, one_or_three_on, backwards=True))
    far_two = wide_sum(two_f, core[1])
    two_n, dq_far = after((two_n, dq_far), far_two)
    far_two = routed(far_two, two_on, backwards=True)
    dq_last = swap(dq_far, "head")
    near_two = routed(wide_sum(two_n, core[0]), two_on, backwards=True)

    def all_heads(tile):
        return jnp.concatenate([odd[tile] for odd in odds], axis=-1)

    far_total = wide_sum(own_f, all_heads(1), far_two)
    far = swap(far_total, "head")
    near = wide_sum(own_n, all_heads(0), after(near_two, far_total))

    def whole(near, far):
        return jnp.where(mine == 0, jnp.concatenate(near + far, -1), jnp.concatenate(far + near, -1))

    both = whole([near], [far])
    half = pl.BlockSpec((rows, width), lambda i, mine: (0, 1 - mine[0]))
    dq = pl.pallas_call(
        fill_kernel,
        out_shape=jax.ShapeDtypeStruct(queries.shape, jnp.bfloat16),
        grid_spec=pltpu.PrefetchScalarGridSpec(
            num_scalar_prefetch=1,
            grid=(1,),
            in_specs=[pl.BlockSpec(dq_first.shape, lambda i, mine: (0, 0))] * PARTS
            + [pl.BlockSpec(memory_space=pl.ANY)],
            out_specs=half,
        ),
        input_output_aliases={3: 0},
        compiler_params=pltpu.CompilerParams(vmem_limit_bytes=SMALL_LIMIT),
        cost_estimate=pl.CostEstimate(flops=DQ_COST, bytes_accessed=1, transcendentals=0),
        name="fill_in",
    )(lists[0], dq_first, dq_last, dq_near)
    return dq, both[0], both[1]


def per_device(queries, keys, values, out_grad, log_norm, row_delta, tile_pairs, pair_count):
    heads = lax.axis_size("head")
    local_kv = keys.shape[1] // heads // HEAD_DIM
    group = queries.shape[1] // keys.shape[1]
    paired = heads == 2 and queries.shape[0] == TILE and local_kv % PARTS == 0 and group % 2 == 0
    form = by_pairs if paired else by_blocks
    return form(queries, keys, values, out_grad, log_norm, row_delta, tile_pairs, pair_count)


def solution(mesh):
    rows = P(("ctx", "head"), None)
    return jax.shard_map(
        per_device,
        mesh=mesh,
        in_specs=(rows,) * 6 + (P("ctx", None, None, None), P("ctx", None)),
        out_specs=(rows,) * 3,
        check_vma=False,
    )
```

```python
import functools

import jax
import jax.numpy as jnp
from jax import lax
from jax.experimental import pallas as pl
from jax.experimental.pallas import tpu as pltpu
from jax.sharding import PartitionSpec as P

HEAD_DIM = 128
TILE = 128
WIN = 4
LOG2E = 1.4426950408889634
FAR = 1e30
PARTS = 2
TOUCH_COST = 6000000000
VMEM_LIMIT = 20 * 1024 * 1024
SMALL_LIMIT = 60 * 1024 * 1024
FIRST_COST, SECOND_COST, DQ_COST, PACK_COST = 1000, 10000000000, 1000, 1000
NT = (((1,), (1,)), ((), ()))
NN = (((1,), (0,)), ((), ()))


def dot(a, b, dims):
    return lax.dot_general(a, b, dims, preferred_element_type=jnp.float32)


def swap(value, axis):
    return lax.ppermute(value, axis, [(i, i ^ 1) for i in range(lax.axis_size(axis))])


def routed(value, route, backwards=False):
    count = lax.axis_size("ctx")
    pairs = [(c, route(c)) for c in range(count) if route(c) < count]
    if backwards:
        pairs = [(b, a) for a, b in pairs]
    return lax.ppermute(value, "ctx", pairs)


def two_on(c):
    return c + 2


def one_or_three_on(c):
    return c + 1 if c % 2 == 0 else c + 3


def mark_live(tiles, slots, turn, steps, pairs, counts, live):
    def clear(i, _):
        live[i] = 0
        return _

    lax.fori_loop(0, WIN * tiles * tiles, clear, 0)
    for b, step in steps:

        def mark(slot, _, b=b, step=step):
            q_at, k_at = pairs[0, step, 0, slot], pairs[0, step, 1, slot]
            if tiles == 2:
                q_at, k_at = (q_at + turn) % 2, (k_at + turn) % 2
            live[(b * tiles + k_at) * tiles + q_at] = 1
            return _

        lax.fori_loop(0, counts[0, step], mark, 0)


def block_kernel(tiles, group, slots, *refs):
    pairs, counts, q_all, g_all, rows_ref, kv_own, kv_two, kv_core, kv_odd = refs[:9]
    dq_ref, d_own, d_two, d_core, d_odd, live, k_rows, v_rows, k_cols, dk_sum, dv_sum = refs[9:]
    scale = HEAD_DIM**-0.5
    odd = lax.axis_index("ctx") % 2
    block = tiles * TILE
    chunk = 2 * TILE
    steps = enumerate((0, 2, 1 + 2 * odd, 3 - 2 * odd))
    mark_live(tiles, slots, 0, steps, pairs, counts, live)
    for b, ref in enumerate((kv_own, kv_two, kv_core, kv_odd)):
        for t in range(tiles):
            at = pl.ds(b * block + t * TILE, TILE)
            k_rows[at, :] = ref[t, 0]
            v_rows[at, :] = ref[t, 1]
            k_cols[:, at] = ref[t, 0].T
    below = lax.broadcasted_iota(jnp.int32, (TILE, 2 * TILE), 0)
    across = lax.broadcasted_iota(jnp.int32, (TILE, 2 * TILE), 1) % TILE
    causal = below <= across

    for t in range(tiles):
        for pair in range(group // 2):
            first = t == 0 and pair == 0
            cut = pl.ds(pair * 2 * HEAD_DIM, HEAD_DIM), pl.ds((pair * 2 + 1) * HEAD_DIM, HEAD_DIM)
            q_two = jnp.concatenate([q_all[t, :, cut[0]], q_all[t, :, cut[1]]], axis=0)
            g_two = jnp.concatenate([g_all[t, :, cut[0]], g_all[t, :, cut[1]]], axis=0)
            norm = [rows_ref[t, 0, 0, pl.ds(pair * 2 + i, 1), :] for i in range(2)]
            delta = [rows_ref[t, 1, 0, pl.ds(pair * 2 + i, 1), :] for i in range(2)]
            norm = jnp.concatenate(norm, axis=1) * LOG2E
            delta = jnp.concatenate(delta, axis=1)

            def one_chunk(n, dq, t=t, first=first, q_two=q_two, g_two=g_two, norm=norm, delta=delta):
                at = pl.ds(pl.multiple_of(n * chunk, chunk), chunk)
                scores = dot(k_rows[at, :], q_two, NT) * (scale * LOG2E)
                prob_grad = dot(v_rows[at, :], g_two, NT)
                probs, grads = [], []
                for half in range(2):
                    k_at = n * 2 + half
                    part = slice(half * TILE, (half + 1) * TILE)
                    shift = jnp.where(live[k_at * tiles + t] > 0, norm, FAR)
                    power = jnp.where(causal | (k_at != t), scores[part] - shift, -FAR)
                    prob = jnp.exp2(power)
                    probs.append(prob.astype(jnp.bfloat16))
                    grads.append((prob * (prob_grad[part] - delta)).astype(jnp.bfloat16))
                probs = jnp.concatenate(probs, axis=0)
                grads = jnp.concatenate(grads, axis=0)
                dv = dot(probs, g_two, NN)
                dk = dot(grads, q_two, NN)
                if first:
                    dv_sum[at, :] = dv
                    dk_sum[at, :] = dk
                else:
                    dv_sum[at, :] += dv
                    dk_sum[at, :] += dk
                return dq + dot(k_cols[:, at], grads, NN)

            dq = jnp.zeros((HEAD_DIM, 2 * TILE), jnp.float32)
            dq = lax.fori_loop(0, WIN * block // chunk, one_chunk, dq)
            dq = ((dq * scale).T).astype(jnp.bfloat16)
            dq_ref[t, :, cut[0]] = dq[:TILE]
            dq_ref[t, :, cut[1]] = dq[TILE:]

    for b, ref in enumerate((d_own, d_two, d_core, d_odd)):
        for t in range(tiles):
            at = pl.ds(b * block + t * TILE, TILE)
            ref[t, 0] = (dk_sum[at, :] * scale).astype(ref.dtype)
            ref[t, 1] = dv_sum[at, :].astype(ref.dtype)


def pair_kernel(part, group, slots, blocks, n_unused, *refs):
    refs = list(refs)
    mine, pairs, counts, q_mine, q_far, g_mine, g_far, rows_mine, rows_far = refs[:9]
    del refs[:9]
    sources = {}
    for b in blocks:
        sources[b] = tuple(refs[: 3 if b == 0 else 2])
        del refs[: len(sources[b])]
    del refs[:n_unused]
    dq_outs = (refs.pop(0), refs.pop(0))
    outs = {}
    for b in blocks:
        first = refs.pop(0)
        outs[b] = (first.at[0], first.at[1]) if b == 2 else (first, refs.pop(0))
    live, k_cols, prob_all, grad_all = refs[-4:]
    scale = HEAD_DIM**-0.5
    odd = lax.axis_index("ctx") % 2
    block = 2 * TILE
    units = [(t, pair) for t in range(2) for pair in range(group // 2)]
    step_of = (0, 2, 1 + 2 * odd, 3 - 2 * odd)
    mark_live(2, slots, mine[0], [(b, step_of[b]) for b in blocks], pairs, counts, live)

    below = lax.broadcasted_iota(jnp.int32, (TILE, 2 * TILE), 0)
    across = lax.broadcasted_iota(jnp.int32, (TILE, 2 * TILE), 1) % TILE
    causal = below <= across
    sides = ((q_mine, g_mine), (q_far, g_far))

    def heads_of(ref):
        return [ref[:, i * HEAD_DIM : (i + 1) * HEAD_DIM] for i in range(group)]

    q_all = jnp.concatenate([x for q, g in sides for x in heads_of(q)], axis=0)
    g_all = jnp.concatenate([x for q, g in sides for x in heads_of(g)], axis=0)
    far = rows_far[...].astype(jnp.float32)
    far = sum(far[:, part * 3 + i : part * 3 + i + 1] for i in range(3))
    rows = []
    for t, pair in units:
        at = slice(pair * block, (pair + 1) * block)
        norm, delta = [(rows_mine[i, :, at], far[i, :, at])[t] for i in range(2)]
        rows.append((norm * LOG2E, delta))

    for n, b in enumerate(blocks):
        if b == 0:
            k_mine, v_mine, kv_far = sources[b]
            k = jnp.concatenate([k_mine[...], kv_far[0]], axis=0)
            v = jnp.concatenate([v_mine[...], kv_far[1]], axis=0)
        else:
            kv_near, kv_far = sources[b]
            k = jnp.concatenate([kv_near[0], kv_far[0]], axis=0)
            v = jnp.concatenate([kv_near[1], kv_far[1]], axis=0)
        at = slice(n * block, (n + 1) * block)
        k_cols[:, at] = k.T
        for u, (t, pair) in enumerate(units):
            cut = slice(u * block, (u + 1) * block)
            norm, delta = rows[u]
            scores = dot(k, q_all[cut], NT) * (scale * LOG2E)
            prob_grad = dot(v, g_all[cut], NT)
            for k_at in range(2):
                part = slice(k_at * TILE, (k_at + 1) * TILE)
                shift = jnp.where(live[(b * 2 + k_at) * 2 + t] > 0, norm, FAR)
                power = scores[part] - shift
                if b == 0 and k_at == t:
                    power = jnp.where(causal, power, -FAR)
                prob = jnp.exp2(power)
                to = slice(n * block + k_at * TILE, n * block + (k_at + 1) * TILE)
                prob_all[to, cut] = prob.astype(jnp.bfloat16)
                grad_all[to, cut] = (prob * (prob_grad[part] - delta)).astype(jnp.bfloat16)
        dv = dot(prob_all[at, :], g_all, NN)
        dk = dot(grad_all[at, :], q_all, NN) * scale
        for t, out in enumerate(outs[b]):
            part = slice(t * TILE, (t + 1) * TILE)
            out[0] = dk[part].astype(out.dtype)
            out[1] = dv[part].astype(out.dtype)

    for u, (t, pair) in enumerate(units):
        cut = slice(u * block, (u + 1) * block)
        dq = dot(k_cols[...], grad_all[:, cut], NN)
        dq = (dq * scale).T.astype(jnp.bfloat16)
        for i in range(2):
            head = pair * 2 + i
            dq_outs[t][:, head * HEAD_DIM : (head + 1) * HEAD_DIM] = dq[i * TILE : (i + 1) * TILE]


def by_blocks(queries, keys, values, out_grad, log_norm, row_delta, tile_pairs, pair_count):
    heads = lax.axis_size("head")
    rows = queries.shape[0]
    width = queries.shape[1] // heads
    kv_width = keys.shape[1] // heads
    local_kv = kv_width // HEAD_DIM
    group = width // kv_width
    tiles = heads * rows // TILE
    per = rows // TILE

    def spread(x, split_at):
        return lax.all_to_all(x, "head", split_axis=split_at, concat_axis=0)

    kv_own = spread(jnp.stack([keys, values]).reshape(2, rows, heads, kv_width), 2)
    kv_own = jnp.swapaxes(kv_own.reshape(heads, 2, per, TILE, kv_width), 1, 2)
    kv_own = kv_own.reshape(tiles, 2, TILE, kv_width)
    q_all = spread(queries.reshape(rows, heads, width), 1).reshape(tiles, TILE, width)
    g_all = spread(out_grad.reshape(rows, heads, width), 1).reshape(tiles, TILE, width)
    small = jnp.stack([log_norm.T, row_delta.T]).reshape(2, heads, local_kv, group, rows)
    small = spread(small, 1).reshape(heads, 2, local_kv, group, per, TILE)
    small = jnp.moveaxis(small, 4, 1).reshape(tiles, 2, local_kv, group, TILE)

    kv_two = routed(kv_own, two_on)
    kv_odd = routed(kv_own, one_or_three_on)
    kv_core = swap(kv_two, "ctx")

    kv_spec = pl.BlockSpec((tiles, 2, TILE, HEAD_DIM), lambda h, *_: (0, 0, 0, h))
    q_spec = pl.BlockSpec((tiles, TILE, group * HEAD_DIM), lambda h, *_: (0, 0, h))
    small_spec = pl.BlockSpec((tiles, 2, 1, group, TILE), lambda h, *_: (0, 0, h, 0, 0))
    keys_all = WIN * tiles * TILE
    kinds = (jnp.float32, jnp.float32, jnp.bfloat16, jnp.bfloat16)
    dq, d_own, d_two, d_core, d_odd = pl.pallas_call(
        functools.partial(block_kernel, tiles, group, tile_pairs.shape[2]),
        out_shape=[jax.ShapeDtypeStruct(q_all.shape, jnp.bfloat16)]
        + [jax.ShapeDtypeStruct(kv_own.shape, t) for t in kinds],
        grid_spec=pltpu.PrefetchScalarGridSpec(
            num_scalar_prefetch=2,
            grid=(local_kv,),
            in_specs=[q_spec, q_spec, small_spec] + [kv_spec] * 4,
            out_specs=[q_spec] + [kv_spec] * 4,
            scratch_shapes=[
                pltpu.SMEM((WIN * tiles * tiles,), jnp.int32),
                pltpu.VMEM((keys_all, HEAD_DIM), jnp.bfloat16),
                pltpu.VMEM((keys_all, HEAD_DIM), jnp.bfloat16),
                pltpu.VMEM((HEAD_DIM, keys_all), jnp.bfloat16),
                pltpu.VMEM((keys_all, HEAD_DIM), jnp.float32),
                pltpu.VMEM((keys_all, HEAD_DIM), jnp.float32),
            ],
        ),
        compiler_params=pltpu.CompilerParams(vmem_limit_bytes=48 * 1024 * 1024),
        name="block_grads",
    )(jnp.swapaxes(tile_pairs, 2, 3), pair_count, q_all, g_all, small, kv_own, kv_two, kv_core, kv_odd)
    d_all = home(d_own, d_two, d_core, d_odd)
    dq = lax.all_to_all(dq.reshape(heads, rows, width), "head", split_axis=0, concat_axis=1)
    d_all = jnp.swapaxes(d_all.reshape(heads, per, 2, TILE, kv_width), 1, 2)
    d_all = d_all.reshape(heads, 2, rows, kv_width)
    d_all = lax.all_to_all(d_all, "head", split_axis=0, concat_axis=2).reshape(2, *keys.shape)
    return dq.reshape(queries.shape), d_all[0], d_all[1]


def home(d_own, d_two, d_core, d_odd):
    from_odd = routed(d_odd, one_or_three_on, backwards=True)
    d_two = d_two + swap(d_core, "ctx").astype(jnp.float32)
    from_two = routed(d_two.astype(jnp.bfloat16), two_on, backwards=True)
    total = d_own + from_odd.astype(jnp.float32) + from_two.astype(jnp.float32)
    return total.astype(jnp.bfloat16)


def then(value, *before):
    return lax.optimization_barrier((value, *before))[0]


def pack_kernel(heads, mine, q_far, g_far, norm, delta, *outs):
    *parts, rows = outs
    size = parts[0].shape[2]
    tile = q_far.shape[0]
    for p, part in enumerate(parts):
        cut = slice(p * size, (p + 1) * size)
        part[0, :tile] = q_far[:, cut]
        part[1, :tile] = g_far[:, cut]
    for i, ref in enumerate((norm, delta)):
        both = ref[...]
        low_side = mine[0] == 0
        own = jnp.where(low_side, both[:heads], both[heads:])
        other = jnp.where(low_side, both[heads:], both[:heads])
        high = other.astype(jnp.bfloat16)
        rest = other - high.astype(jnp.float32)
        middle = rest.astype(jnp.bfloat16)
        low = (rest - middle.astype(jnp.float32)).astype(jnp.bfloat16)
        for h in range(heads):
            rows[i, :, h * tile : (h + 1) * tile] = own[h : h + 1]
        per = size // tile
        pad = [jnp.zeros((16 - 3 * len(parts), tile), jnp.float32)]
        for at in range(per):
            heads_at = [at + p * per for p in range(len(parts))]
            three = [x[h : h + 1].astype(jnp.float32) for h in heads_at for x in (high, middle, low)]
            block = jnp.concatenate(three + pad, axis=0).astype(jnp.bfloat16)
            parts[0][i, tile:, at * tile : (at + 1) * tile] = block


def fill_kernel(mine, first, last, before, half):
    size = first.shape[1]
    half[:, :size] = first[...]
    half[:, size:] = last[...]


def after(value, *before):
    return lax.optimization_barrier((value, *before))[0]


def touch_kernel(x_ref, y_ref, mark):
    mark[0] = 1


def touch(x, cost):
    return pl.pallas_call(
        touch_kernel,
        out_shape=jax.ShapeDtypeStruct(x.shape, x.dtype),
        in_specs=[pl.BlockSpec(memory_space=pl.ANY)],
        out_specs=pl.BlockSpec(memory_space=pl.ANY),
        input_output_aliases={0: 0},
        scratch_shapes=[pltpu.SMEM((1,), jnp.int32)],
        cost_estimate=pl.CostEstimate(flops=cost, bytes_accessed=1, transcendentals=0),
        name="arrived",
    )(x)


def by_pairs(queries, keys, values, out_grad, log_norm, row_delta, tile_pairs, pair_count):
    mine = lax.axis_index("head")
    rows = queries.shape[0]
    width = queries.shape[1] // 2
    kv_width = keys.shape[1] // 2
    local_kv = kv_width // HEAD_DIM
    group = width // kv_width
    kvs = local_kv // PARTS
    wide = group * HEAD_DIM
    lists = (mine.reshape(1), jnp.swapaxes(tile_pairs, 2, 3), pair_count)

    def cut(x, side):
        size = x.shape[1] // 2
        return lax.dynamic_slice_in_dim(x, side * size, size, 1)

    kv_near = jnp.stack([cut(keys, mine), cut(values, mine)])
    kv_far = swap(jnp.stack([cut(keys, 1 - mine), cut(values, 1 - mine)]), "head")
    kv_far = touch(kv_far, TOUCH_COST)
    pack_spec = pl.BlockSpec((rows, width), lambda i, mine: (0, 1 - mine[0]))
    whole_spec = pl.BlockSpec((2 * local_kv * group, rows), lambda i, mine: (0, 0))
    packed = [(2, rows + (16 if part == 0 else 0), kvs * wide) for part in range(PARTS)]
    *qg_send, small = pl.pallas_call(
        functools.partial(pack_kernel, local_kv * group),
        out_shape=[pltpu.HBM(s, jnp.bfloat16) for s in packed]
        + [jax.ShapeDtypeStruct((2, 1, width), jnp.float32)],
        grid_spec=pltpu.PrefetchScalarGridSpec(
            num_scalar_prefetch=1,
            grid=(1,),
            in_specs=[pack_spec, pack_spec, whole_spec, whole_spec],
            out_specs=[pl.BlockSpec(s, lambda i, mine: (0, 0, 0)) for s in packed + [(2, 1, width)]],
        ),
        compiler_params=pltpu.CompilerParams(vmem_limit_bytes=SMALL_LIMIT),
        cost_estimate=pl.CostEstimate(flops=PACK_COST, bytes_accessed=1, transcendentals=0),
        name="pack_sends",
    )(lists[0], queries, out_grad, log_norm.T, row_delta.T)
    qg_far = [swap(x, "head") for x in qg_send]
    near_two, near_odd = routed(kv_near, two_on), routed(after(kv_near, kv_far), one_or_three_on)
    far_two, far_odd = routed(kv_far, two_on), routed(kv_far, one_or_three_on)
    near_core = swap(near_two, "ctx")

    def attend(part, blocks, sources, before, cost):
        first = part * kvs

        def at_mine(h, mine, *_):
            return (0, mine[0] * local_kv + first + h)

        q_own = pl.BlockSpec((rows, wide), at_mine)
        k_own = pl.BlockSpec((rows, HEAD_DIM), at_mine)
        far = lambda i: pl.BlockSpec((None, rows, wide), lambda h, *_: (i, 0, h))
        kv_spec = pl.BlockSpec((2, rows, HEAD_DIM), lambda h, *_: (0, 0, first + h))
        args = [queries, qg_far[part], out_grad, qg_far[part], small, qg_far[0]]
        specs = [
            q_own,
            far(0),
            q_own,
            far(1),
            pl.BlockSpec((2, 1, wide), lambda h, *_: (0, 0, first + h)),
            pl.BlockSpec((2, 16, wide), lambda h, *_: (0, rows // 16, h)),
        ]
        for b in blocks:
            args += sources[b]
            specs += [k_own, k_own, kv_spec] if b == 0 else [kv_spec, kv_spec]
        dq_shapes = [queries.shape, (rows, kvs * wide)]
        outs = [pltpu.HBM(s, jnp.bfloat16) for s in dq_shapes]
        out_specs = [q_own, pl.BlockSpec((rows, wide), lambda h, *_: (0, h))]
        kinds = (jnp.float32, jnp.float32, jnp.bfloat16, jnp.bfloat16)
        both_spec = pl.BlockSpec((2, 2, rows, HEAD_DIM), lambda h, *_: (0, 0, 0, first + h))
        for b in blocks:
            if b == 2:
                outs.append(pltpu.HBM((2, 2, rows, kv_width), kinds[b]))
                out_specs.append(both_spec)
            else:
                outs += [pltpu.HBM((2, rows, kv_width), kinds[b])] * 2
                out_specs += [kv_spec] * 2
        alias, n_args = {}, len(args)
        if before is not None:
            for i, array in enumerate(before):
                alias[len(lists) + len(args)] = i if i == 0 else i + 1
                args.append(array)
        specs += [pl.BlockSpec(memory_space=pl.ANY)] * (len(args) - n_args)
        keys_all = len(blocks) * 2 * TILE
        return pl.pallas_call(
            functools.partial(
                pair_kernel,
                part,
                group,
                tile_pairs.shape[2],
                blocks,
                len(args) - n_args,
            ),
            out_shape=outs,
            grid_spec=pltpu.PrefetchScalarGridSpec(
                num_scalar_prefetch=3,
                grid=(kvs,),
                in_specs=specs,
                out_specs=out_specs,
                scratch_shapes=[
                    pltpu.SMEM((WIN * 4,), jnp.int32),
                    pltpu.VMEM((HEAD_DIM, keys_all), jnp.bfloat16),
                    pltpu.VMEM((keys_all, 2 * group * TILE), jnp.bfloat16),
                    pltpu.VMEM((keys_all, 2 * group * TILE), jnp.bfloat16),
                ],
            ),
            input_output_aliases=alias,
            compiler_params=pltpu.CompilerParams(vmem_limit_bytes=VMEM_LIMIT),
            cost_estimate=pl.CostEstimate(flops=cost, bytes_accessed=1, transcendentals=0),
            name="grads_" + "".join(map(str, blocks)) + "_part" + str(part),
        )(*lists, *args)

    sources = {
        0: (keys, values, kv_far),
        1: (near_two, far_two),
        2: (near_core, swap(after(far_two, near_odd), "ctx")),
        3: (near_odd, far_odd),
    }
    def wide_sum(*terms):
        return sum(x.astype(jnp.float32) for x in terms).astype(jnp.bfloat16)

    blocks = (0, 1, 2, 3)
    dq_near, dq_far, *sums = attend(0, blocks, sources, None, FIRST_COST)
    dq_before = dq_far
    dq_near, dq_far, *sums = attend(1, blocks, sources, (dq_near, *sums), SECOND_COST)
    own_n, own_f, two_n, two_f, core, odd_n, odd_f = sums
    core = swap(core, "ctx")
    dq_first = swap(after(dq_before, dq_far), "head")
    far_odd = routed(odd_f, one_or_three_on, backwards=True)
    far_two = wide_sum(two_f, core[1])
    odd_n, two_n, dq_far = after((odd_n, two_n, dq_far), far_two)
    far_two = routed(far_two, two_on, backwards=True)
    dq_last = swap(dq_far, "head")
    near_odd = routed(odd_n, one_or_three_on, backwards=True)
    near_two = routed(wide_sum(after(two_n, dq_first), core[0]), two_on, backwards=True)
    far = swap(wide_sum(own_f, far_odd, far_two), "head")
    near = wide_sum(own_n, near_odd, near_two)

    def whole(near, far):
        return jnp.where(mine == 0, jnp.concatenate(near + far, -1), jnp.concatenate(far + near, -1))

    both = whole([near], [far])
    half = pl.BlockSpec((rows, width), lambda i, mine: (0, 1 - mine[0]))
    dq = pl.pallas_call(
        fill_kernel,
        out_shape=jax.ShapeDtypeStruct(queries.shape, jnp.bfloat16),
        grid_spec=pltpu.PrefetchScalarGridSpec(
            num_scalar_prefetch=1,
            grid=(1,),
            in_specs=[pl.BlockSpec(dq_first.shape, lambda i, mine: (0, 0))] * PARTS
            + [pl.BlockSpec(memory_space=pl.ANY)],
            out_specs=half,
        ),
        input_output_aliases={3: 0},
        compiler_params=pltpu.CompilerParams(vmem_limit_bytes=SMALL_LIMIT),
        cost_estimate=pl.CostEstimate(flops=DQ_COST, bytes_accessed=1, transcendentals=0),
        name="fill_in",
    )(lists[0], dq_first, dq_last, dq_near)
    return dq, both[0], both[1]


def per_device(queries, keys, values, out_grad, log_norm, row_delta, tile_pairs, pair_count):
    heads = lax.axis_size("head")
    local_kv = keys.shape[1] // heads // HEAD_DIM
    group = queries.shape[1] // keys.shape[1]
    paired = heads == 2 and queries.shape[0] == TILE and local_kv % PARTS == 0 and group % 2 == 0
    form = by_pairs if paired else by_blocks
    return form(queries, keys, values, out_grad, log_norm, row_delta, tile_pairs, pair_count)


def solution(mesh):
    rows = P(("ctx", "head"), None)
    return jax.shard_map(
        per_device,
        mesh=mesh,
        in_specs=(rows,) * 6 + (P("ctx", None, None, None), P("ctx", None)),
        out_specs=(rows,) * 3,
        check_vma=False,
    )
```

```python
import functools

import jax
import jax.numpy as jnp
from jax import lax
from jax.experimental import pallas as pl
from jax.experimental.pallas import tpu as pltpu
from jax.sharding import PartitionSpec as P

HEAD_DIM = 128
TILE = 128
WIN = 4
LOG2E = 1.4426950408889634
FAR = 1e30
PARTS = 2
TOUCH_COST = 6000000000
VMEM_LIMIT = 20 * 1024 * 1024
SMALL_LIMIT = 60 * 1024 * 1024
FIRST_COST, SECOND_COST, DQ_COST, PACK_COST = 1000, 10000000000, 1000, 1000
NT = (((1,), (1,)), ((), ()))
NN = (((1,), (0,)), ((), ()))


def dot(a, b, dims):
    return lax.dot_general(a, b, dims, preferred_element_type=jnp.float32)


def swap(value, axis):
    return lax.ppermute(value, axis, [(i, i ^ 1) for i in range(lax.axis_size(axis))])


def routed(value, route, backwards=False):
    count = lax.axis_size("ctx")
    pairs = [(c, route(c)) for c in range(count) if route(c) < count]
    if backwards:
        pairs = [(b, a) for a, b in pairs]
    return lax.ppermute(value, "ctx", pairs)


def two_on(c):
    return c + 2


def one_or_three_on(c):
    return c + 1 if c % 2 == 0 else c + 3


def mark_live(tiles, slots, turn, steps, pairs, counts, live):
    def clear(i, _):
        live[i] = 0
        return _

    lax.fori_loop(0, WIN * tiles * tiles, clear, 0)
    for b, step in steps:

        def mark(slot, _, b=b, step=step):
            q_at, k_at = pairs[0, step, 0, slot], pairs[0, step, 1, slot]
            if tiles == 2:
                q_at, k_at = (q_at + turn) % 2, (k_at + turn) % 2
            live[(b * tiles + k_at) * tiles + q_at] = 1
            return _

        lax.fori_loop(0, counts[0, step], mark, 0)


def block_kernel(tiles, group, slots, *refs):
    pairs, counts, q_all, g_all, rows_ref, kv_own, kv_two, kv_core, kv_odd = refs[:9]
    dq_ref, d_own, d_two, d_core, d_odd, live, k_rows, v_rows, k_cols, dk_sum, dv_sum = refs[9:]
    scale = HEAD_DIM**-0.5
    odd = lax.axis_index("ctx") % 2
    block = tiles * TILE
    chunk = 2 * TILE
    steps = enumerate((0, 2, 1 + 2 * odd, 3 - 2 * odd))
    mark_live(tiles, slots, 0, steps, pairs, counts, live)
    for b, ref in enumerate((kv_own, kv_two, kv_core, kv_odd)):
        for t in range(tiles):
            at = pl.ds(b * block + t * TILE, TILE)
            k_rows[at, :] = ref[t, 0]
            v_rows[at, :] = ref[t, 1]
            k_cols[:, at] = ref[t, 0].T
    below = lax.broadcasted_iota(jnp.int32, (TILE, 2 * TILE), 0)
    across = lax.broadcasted_iota(jnp.int32, (TILE, 2 * TILE), 1) % TILE
    causal = below <= across

    for t in range(tiles):
        for pair in range(group // 2):
            first = t == 0 and pair == 0
            cut = pl.ds(pair * 2 * HEAD_DIM, HEAD_DIM), pl.ds((pair * 2 + 1) * HEAD_DIM, HEAD_DIM)
            q_two = jnp.concatenate([q_all[t, :, cut[0]], q_all[t, :, cut[1]]], axis=0)
            g_two = jnp.concatenate([g_all[t, :, cut[0]], g_all[t, :, cut[1]]], axis=0)
            norm = [rows_ref[t, 0, 0, pl.ds(pair * 2 + i, 1), :] for i in range(2)]
            delta = [rows_ref[t, 1, 0, pl.ds(pair * 2 + i, 1), :] for i in range(2)]
            norm = jnp.concatenate(norm, axis=1) * LOG2E
            delta = jnp.concatenate(delta, axis=1)

            def one_chunk(n, dq, t=t, first=first, q_two=q_two, g_two=g_two, norm=norm, delta=delta):
                at = pl.ds(pl.multiple_of(n * chunk, chunk), chunk)
                scores = dot(k_rows[at, :], q_two, NT) * (scale * LOG2E)
                prob_grad = dot(v_rows[at, :], g_two, NT)
                probs, grads = [], []
                for half in range(2):
                    k_at = n * 2 + half
                    part = slice(half * TILE, (half + 1) * TILE)
                    shift = jnp.where(live[k_at * tiles + t] > 0, norm, FAR)
                    power = jnp.where(causal | (k_at != t), scores[part] - shift, -FAR)
                    prob = jnp.exp2(power)
                    probs.append(prob.astype(jnp.bfloat16))
                    grads.append((prob * (prob_grad[part] - delta)).astype(jnp.bfloat16))
                probs = jnp.concatenate(probs, axis=0)
                grads = jnp.concatenate(grads, axis=0)
                dv = dot(probs, g_two, NN)
                dk = dot(grads, q_two, NN)
                if first:
                    dv_sum[at, :] = dv
                    dk_sum[at, :] = dk
                else:
                    dv_sum[at, :] += dv
                    dk_sum[at, :] += dk
                return dq + dot(k_cols[:, at], grads, NN)

            dq = jnp.zeros((HEAD_DIM, 2 * TILE), jnp.float32)
            dq = lax.fori_loop(0, WIN * block // chunk, one_chunk, dq)
            dq = ((dq * scale).T).astype(jnp.bfloat16)
            dq_ref[t, :, cut[0]] = dq[:TILE]
            dq_ref[t, :, cut[1]] = dq[TILE:]

    for b, ref in enumerate((d_own, d_two, d_core, d_odd)):
        for t in range(tiles):
            at = pl.ds(b * block + t * TILE, TILE)
            ref[t, 0] = (dk_sum[at, :] * scale).astype(ref.dtype)
            ref[t, 1] = dv_sum[at, :].astype(ref.dtype)


def pair_kernel(part, group, slots, blocks, n_unused, *refs):
    refs = list(refs)
    mine, pairs, counts, q_mine, q_far, g_mine, g_far, rows_mine, rows_far = refs[:9]
    del refs[:9]
    sources = {}
    for b in blocks:
        sources[b] = tuple(refs[: 3 if b == 0 else 2])
        del refs[: len(sources[b])]
    del refs[:n_unused]
    dq_outs = (refs.pop(0), refs.pop(0))
    outs = {}
    for b in blocks:
        first = refs.pop(0)
        outs[b] = (first.at[0], first.at[1]) if b == 2 else (first, refs.pop(0))
    live, k_cols, prob_all, grad_all = refs[-4:]
    scale = HEAD_DIM**-0.5
    odd = lax.axis_index("ctx") % 2
    block = 2 * TILE
    units = [(t, pair) for t in range(2) for pair in range(group // 2)]
    step_of = (0, 2, 1 + 2 * odd, 3 - 2 * odd)
    mark_live(2, slots, mine[0], [(b, step_of[b]) for b in blocks], pairs, counts, live)

    below = lax.broadcasted_iota(jnp.int32, (TILE, 2 * TILE), 0)
    across = lax.broadcasted_iota(jnp.int32, (TILE, 2 * TILE), 1) % TILE
    causal = below <= across
    sides = ((q_mine, g_mine), (q_far, g_far))

    def heads_of(ref):
        return [ref[:, i * HEAD_DIM : (i + 1) * HEAD_DIM] for i in range(group)]

    q_all = jnp.concatenate([x for q, g in sides for x in heads_of(q)], axis=0)
    g_all = jnp.concatenate([x for q, g in sides for x in heads_of(g)], axis=0)
    far = rows_far[...].astype(jnp.float32)
    far = sum(far[:, part * 3 + i : part * 3 + i + 1] for i in range(3))
    rows = []
    for t, pair in units:
        at = slice(pair * block, (pair + 1) * block)
        norm, delta = [(rows_mine[i, :, at], far[i, :, at])[t] for i in range(2)]
        rows.append((norm * LOG2E, delta))

    for n, b in enumerate(blocks):
        if b == 0:
            k_mine, v_mine, kv_far = sources[b]
            k = jnp.concatenate([k_mine[...], kv_far[0]], axis=0)
            v = jnp.concatenate([v_mine[...], kv_far[1]], axis=0)
        else:
            kv_near, kv_far = sources[b]
            k = jnp.concatenate([kv_near[0], kv_far[0]], axis=0)
            v = jnp.concatenate([kv_near[1], kv_far[1]], axis=0)
        at = slice(n * block, (n + 1) * block)
        k_cols[:, at] = k.T
        for u, (t, pair) in enumerate(units):
            cut = slice(u * block, (u + 1) * block)
            norm, delta = rows[u]
            scores = dot(k, q_all[cut], NT) * (scale * LOG2E)
            prob_grad = dot(v, g_all[cut], NT)
            for k_at in range(2):
                part = slice(k_at * TILE, (k_at + 1) * TILE)
                shift = jnp.where(live[(b * 2 + k_at) * 2 + t] > 0, norm, FAR)
                power = scores[part] - shift
                if b == 0 and k_at == t:
                    power = jnp.where(causal, power, -FAR)
                prob = jnp.exp2(power)
                to = slice(n * block + k_at * TILE, n * block + (k_at + 1) * TILE)
                prob_all[to, cut] = prob.astype(jnp.bfloat16)
                grad_all[to, cut] = (prob * (prob_grad[part] - delta)).astype(jnp.bfloat16)
        dv = dot(prob_all[at, :], g_all, NN)
        dk = dot(grad_all[at, :], q_all, NN) * scale
        for t, out in enumerate(outs[b]):
            part = slice(t * TILE, (t + 1) * TILE)
            out[0] = dk[part].astype(out.dtype)
            out[1] = dv[part].astype(out.dtype)

    for u, (t, pair) in enumerate(units):
        cut = slice(u * block, (u + 1) * block)
        dq = dot(k_cols[...], grad_all[:, cut], NN)
        dq = (dq * scale).T.astype(jnp.bfloat16)
        for i in range(2):
            head = pair * 2 + i
            dq_outs[t][:, head * HEAD_DIM : (head + 1) * HEAD_DIM] = dq[i * TILE : (i + 1) * TILE]


def by_blocks(queries, keys, values, out_grad, log_norm, row_delta, tile_pairs, pair_count):
    heads = lax.axis_size("head")
    rows = queries.shape[0]
    width = queries.shape[1] // heads
    kv_width = keys.shape[1] // heads
    local_kv = kv_width // HEAD_DIM
    group = width // kv_width
    tiles = heads * rows // TILE
    per = rows // TILE

    def spread(x, split_at):
        return lax.all_to_all(x, "head", split_axis=split_at, concat_axis=0)

    kv_own = spread(jnp.stack([keys, values]).reshape(2, rows, heads, kv_width), 2)
    kv_own = jnp.swapaxes(kv_own.reshape(heads, 2, per, TILE, kv_width), 1, 2)
    kv_own = kv_own.reshape(tiles, 2, TILE, kv_width)
    q_all = spread(queries.reshape(rows, heads, width), 1).reshape(tiles, TILE, width)
    g_all = spread(out_grad.reshape(rows, heads, width), 1).reshape(tiles, TILE, width)
    small = jnp.stack([log_norm.T, row_delta.T]).reshape(2, heads, local_kv, group, rows)
    small = spread(small, 1).reshape(heads, 2, local_kv, group, per, TILE)
    small = jnp.moveaxis(small, 4, 1).reshape(tiles, 2, local_kv, group, TILE)

    kv_two = routed(kv_own, two_on)
    kv_odd = routed(kv_own, one_or_three_on)
    kv_core = swap(kv_two, "ctx")

    kv_spec = pl.BlockSpec((tiles, 2, TILE, HEAD_DIM), lambda h, *_: (0, 0, 0, h))
    q_spec = pl.BlockSpec((tiles, TILE, group * HEAD_DIM), lambda h, *_: (0, 0, h))
    small_spec = pl.BlockSpec((tiles, 2, 1, group, TILE), lambda h, *_: (0, 0, h, 0, 0))
    keys_all = WIN * tiles * TILE
    kinds = (jnp.float32, jnp.float32, jnp.bfloat16, jnp.bfloat16)
    dq, d_own, d_two, d_core, d_odd = pl.pallas_call(
        functools.partial(block_kernel, tiles, group, tile_pairs.shape[2]),
        out_shape=[jax.ShapeDtypeStruct(q_all.shape, jnp.bfloat16)]
        + [jax.ShapeDtypeStruct(kv_own.shape, t) for t in kinds],
        grid_spec=pltpu.PrefetchScalarGridSpec(
            num_scalar_prefetch=2,
            grid=(local_kv,),
            in_specs=[q_spec, q_spec, small_spec] + [kv_spec] * 4,
            out_specs=[q_spec] + [kv_spec] * 4,
            scratch_shapes=[
                pltpu.SMEM((WIN * tiles * tiles,), jnp.int32),
                pltpu.VMEM((keys_all, HEAD_DIM), jnp.bfloat16),
                pltpu.VMEM((keys_all, HEAD_DIM), jnp.bfloat16),
                pltpu.VMEM((HEAD_DIM, keys_all), jnp.bfloat16),
                pltpu.VMEM((keys_all, HEAD_DIM), jnp.float32),
                pltpu.VMEM((keys_all, HEAD_DIM), jnp.float32),
            ],
        ),
        compiler_params=pltpu.CompilerParams(vmem_limit_bytes=48 * 1024 * 1024),
        name="block_grads",
    )(jnp.swapaxes(tile_pairs, 2, 3), pair_count, q_all, g_all, small, kv_own, kv_two, kv_core, kv_odd)
    d_all = home(d_own, d_two, d_core, d_odd)
    dq = lax.all_to_all(dq.reshape(heads, rows, width), "head", split_axis=0, concat_axis=1)
    d_all = jnp.swapaxes(d_all.reshape(heads, per, 2, TILE, kv_width), 1, 2)
    d_all = d_all.reshape(heads, 2, rows, kv_width)
    d_all = lax.all_to_all(d_all, "head", split_axis=0, concat_axis=2).reshape(2, *keys.shape)
    return dq.reshape(queries.shape), d_all[0], d_all[1]


def home(d_own, d_two, d_core, d_odd):
    from_odd = routed(d_odd, one_or_three_on, backwards=True)
    d_two = d_two + swap(d_core, "ctx").astype(jnp.float32)
    from_two = routed(d_two.astype(jnp.bfloat16), two_on, backwards=True)
    total = d_own + from_odd.astype(jnp.float32) + from_two.astype(jnp.float32)
    return total.astype(jnp.bfloat16)


def then(value, *before):
    return lax.optimization_barrier((value, *before))[0]


def pack_kernel(heads, mine, q_far, g_far, norm, delta, *outs):
    *parts, rows = outs
    size = parts[0].shape[2]
    tile = q_far.shape[0]
    for p, part in enumerate(parts):
        cut = slice(p * size, (p + 1) * size)
        part[0, :tile] = q_far[:, cut]
        part[1, :tile] = g_far[:, cut]
    for i, ref in enumerate((norm, delta)):
        both = ref[...]
        low_side = mine[0] == 0
        own = jnp.where(low_side, both[:heads], both[heads:])
        other = jnp.where(low_side, both[heads:], both[:heads])
        high = other.astype(jnp.bfloat16)
        rest = other - high.astype(jnp.float32)
        middle = rest.astype(jnp.bfloat16)
        low = (rest - middle.astype(jnp.float32)).astype(jnp.bfloat16)
        for h in range(heads):
            rows[i, :, h * tile : (h + 1) * tile] = own[h : h + 1]
        per = size // tile
        pad = [jnp.zeros((16 - 3 * len(parts), tile), jnp.float32)]
        for at in range(per):
            heads_at = [at + p * per for p in range(len(parts))]
            three = [x[h : h + 1].astype(jnp.float32) for h in heads_at for x in (high, middle, low)]
            block = jnp.concatenate(three + pad, axis=0).astype(jnp.bfloat16)
            parts[0][i, tile:, at * tile : (at + 1) * tile] = block


def fill_kernel(mine, got, before, half):
    half[...] = got[...]


def after(value, *before):
    return lax.optimization_barrier((value, *before))[0]


def touch_kernel(x_ref, y_ref, mark):
    mark[0] = 1


def touch(x, cost):
    return pl.pallas_call(
        touch_kernel,
        out_shape=jax.ShapeDtypeStruct(x.shape, x.dtype),
        in_specs=[pl.BlockSpec(memory_space=pl.ANY)],
        out_specs=pl.BlockSpec(memory_space=pl.ANY),
        input_output_aliases={0: 0},
        scratch_shapes=[pltpu.SMEM((1,), jnp.int32)],
        cost_estimate=pl.CostEstimate(flops=cost, bytes_accessed=1, transcendentals=0),
        name="arrived",
    )(x)


def by_pairs(queries, keys, values, out_grad, log_norm, row_delta, tile_pairs, pair_count):
    mine = lax.axis_index("head")
    rows = queries.shape[0]
    width = queries.shape[1] // 2
    kv_width = keys.shape[1] // 2
    local_kv = kv_width // HEAD_DIM
    group = width // kv_width
    kvs = local_kv // PARTS
    wide = group * HEAD_DIM
    lists = (mine.reshape(1), jnp.swapaxes(tile_pairs, 2, 3), pair_count)

    def cut(x, side):
        size = x.shape[1] // 2
        return lax.dynamic_slice_in_dim(x, side * size, size, 1)

    kv_near = jnp.stack([cut(keys, mine), cut(values, mine)])
    kv_far = swap(jnp.stack([cut(keys, 1 - mine), cut(values, 1 - mine)]), "head")
    kv_far = touch(kv_far, TOUCH_COST)
    pack_spec = pl.BlockSpec((rows, width), lambda i, mine: (0, 1 - mine[0]))
    whole_spec = pl.BlockSpec((2 * local_kv * group, rows), lambda i, mine: (0, 0))
    packed = [(2, rows + (16 if part == 0 else 0), kvs * wide) for part in range(PARTS)]
    *qg_send, small = pl.pallas_call(
        functools.partial(pack_kernel, local_kv * group),
        out_shape=[pltpu.HBM(s, jnp.bfloat16) for s in packed]
        + [jax.ShapeDtypeStruct((2, 1, width), jnp.float32)],
        grid_spec=pltpu.PrefetchScalarGridSpec(
            num_scalar_prefetch=1,
            grid=(1,),
            in_specs=[pack_spec, pack_spec, whole_spec, whole_spec],
            out_specs=[pl.BlockSpec(s, lambda i, mine: (0, 0, 0)) for s in packed + [(2, 1, width)]],
        ),
        compiler_params=pltpu.CompilerParams(vmem_limit_bytes=SMALL_LIMIT),
        cost_estimate=pl.CostEstimate(flops=PACK_COST, bytes_accessed=1, transcendentals=0),
        name="pack_sends",
    )(lists[0], queries, out_grad, log_norm.T, row_delta.T)
    qg_far = [swap(x, "head") for x in qg_send]
    near_two, near_odd = routed(kv_near, two_on), routed(after(kv_near, kv_far), one_or_three_on)
    far_two, far_odd = routed(kv_far, two_on), routed(kv_far, one_or_three_on)
    near_core = swap(near_two, "ctx")

    def attend(part, blocks, sources, before, cost):
        first = part * kvs

        def at_mine(h, mine, *_):
            return (0, mine[0] * local_kv + first + h)

        q_own = pl.BlockSpec((rows, wide), at_mine)
        k_own = pl.BlockSpec((rows, HEAD_DIM), at_mine)
        far = lambda i: pl.BlockSpec((None, rows, wide), lambda h, *_: (i, 0, h))
        kv_spec = pl.BlockSpec((2, rows, HEAD_DIM), lambda h, *_: (0, 0, first + h))
        args = [queries, qg_far[part], out_grad, qg_far[part], small, qg_far[0]]
        specs = [
            q_own,
            far(0),
            q_own,
            far(1),
            pl.BlockSpec((2, 1, wide), lambda h, *_: (0, 0, first + h)),
            pl.BlockSpec((2, 16, wide), lambda h, *_: (0, rows // 16, h)),
        ]
        for b in blocks:
            args += sources[b]
            specs += [k_own, k_own, kv_spec] if b == 0 else [kv_spec, kv_spec]
        dq_shapes = [queries.shape, (rows, width)]
        outs = [pltpu.HBM(s, jnp.bfloat16) for s in dq_shapes]
        out_specs = [q_own, pl.BlockSpec((rows, wide), lambda h, *_: (0, first + h))]
        kinds = (jnp.float32, jnp.float32, jnp.bfloat16, jnp.bfloat16)
        both_spec = pl.BlockSpec((2, 2, rows, HEAD_DIM), lambda h, *_: (0, 0, 0, first + h))
        for b in blocks:
            if b == 2:
                outs.append(pltpu.HBM((2, 2, rows, kv_width), kinds[b]))
                out_specs.append(both_spec)
            else:
                outs += [pltpu.HBM((2, rows, kv_width), kinds[b])] * 2
                out_specs += [kv_spec] * 2
        alias, n_args = {}, len(args)
        if before is not None:
            for i, array in enumerate(before):
                alias[len(lists) + len(args)] = i
                args.append(array)
        specs += [pl.BlockSpec(memory_space=pl.ANY)] * (len(args) - n_args)
        keys_all = len(blocks) * 2 * TILE
        return pl.pallas_call(
            functools.partial(
                pair_kernel,
                part,
                group,
                tile_pairs.shape[2],
                blocks,
                len(args) - n_args,
            ),
            out_shape=outs,
            grid_spec=pltpu.PrefetchScalarGridSpec(
                num_scalar_prefetch=3,
                grid=(kvs,),
                in_specs=specs,
                out_specs=out_specs,
                scratch_shapes=[
                    pltpu.SMEM((WIN * 4,), jnp.int32),
                    pltpu.VMEM((HEAD_DIM, keys_all), jnp.bfloat16),
                    pltpu.VMEM((keys_all, 2 * group * TILE), jnp.bfloat16),
                    pltpu.VMEM((keys_all, 2 * group * TILE), jnp.bfloat16),
                ],
            ),
            input_output_aliases=alias,
            compiler_params=pltpu.CompilerParams(vmem_limit_bytes=VMEM_LIMIT),
            cost_estimate=pl.CostEstimate(flops=cost, bytes_accessed=1, transcendentals=0),
            name="grads_" + "".join(map(str, blocks)) + "_part" + str(part),
        )(*lists, *args)

    sources = {
        0: (keys, values, kv_far),
        1: (near_two, far_two),
        2: (near_core, swap(after(far_two, near_odd), "ctx")),
        3: (near_odd, far_odd),
    }
    def wide_sum(*terms):
        return sum(x.astype(jnp.float32) for x in terms).astype(jnp.bfloat16)

    blocks = (0, 1, 2, 3)
    first = attend(0, blocks, sources, None, FIRST_COST)
    dq_near, dq_far, *sums = attend(1, blocks, sources, first, SECOND_COST)
    own_n, own_f, two_n, two_f, core, odd_n, odd_f = sums
    core = swap(core, "ctx")
    dq_far = swap(dq_far, "head")
    far_odd = routed(odd_f, one_or_three_on, backwards=True)
    far_two = wide_sum(two_f, core[1])
    odd_n, two_n = after((odd_n, two_n), far_two)
    far_two = routed(far_two, two_on, backwards=True)
    near_odd = routed(odd_n, one_or_three_on, backwards=True)
    near_two = routed(wide_sum(two_n, core[0]), two_on, backwards=True)
    far = swap(wide_sum(after(own_f, dq_far), far_odd, far_two), "head")
    near = wide_sum(own_n, near_odd, near_two)

    def whole(near, far):
        return jnp.where(mine == 0, jnp.concatenate(near + far, -1), jnp.concatenate(far + near, -1))

    both = whole([near], [far])
    half = pl.BlockSpec((rows, width), lambda i, mine: (0, 1 - mine[0]))
    dq = pl.pallas_call(
        fill_kernel,
        out_shape=jax.ShapeDtypeStruct(queries.shape, jnp.bfloat16),
        grid_spec=pltpu.PrefetchScalarGridSpec(
            num_scalar_prefetch=1,
            grid=(1,),
            in_specs=[pl.BlockSpec((rows, width), lambda i, mine: (0, 0))]
            + [pl.BlockSpec(memory_space=pl.ANY)],
            out_specs=half,
        ),
        input_output_aliases={2: 0},
        compiler_params=pltpu.CompilerParams(vmem_limit_bytes=SMALL_LIMIT),
        cost_estimate=pl.CostEstimate(flops=DQ_COST, bytes_accessed=1, transcendentals=0),
        name="fill_in",
    )(lists[0], dq_far, dq_near)
    return dq, both[0], both[1]


def per_device(queries, keys, values, out_grad, log_norm, row_delta, tile_pairs, pair_count):
    heads = lax.axis_size("head")
    local_kv = keys.shape[1] // heads // HEAD_DIM
    group = queries.shape[1] // keys.shape[1]
    paired = heads == 2 and queries.shape[0] == TILE and local_kv % PARTS == 0 and group % 2 == 0
    form = by_pairs if paired else by_blocks
    return form(queries, keys, values, out_grad, log_norm, row_delta, tile_pairs, pair_count)


def solution(mesh):
    rows = P(("ctx", "head"), None)
    return jax.shard_map(
        per_device,
        mesh=mesh,
        in_specs=(rows,) * 6 + (P("ctx", None, None, None), P("ctx", None)),
        out_specs=(rows,) * 3,
        check_vma=False,
    )
```

```python
import functools

import jax
import jax.numpy as jnp
from jax import lax
from jax.experimental import pallas as pl
from jax.experimental.pallas import tpu as pltpu
from jax.sharding import PartitionSpec as P

HEAD_DIM = 128
TILE = 128
WIN = 4
LOG2E = 1.4426950408889634
FAR = 1e30
PARTS = 2
TOUCH_COST = 6000000000
VMEM_LIMIT = 20 * 1024 * 1024
SMALL_LIMIT = 60 * 1024 * 1024
FIRST_COST, SECOND_COST, DQ_COST, PACK_COST = 1000, 10000000000, 1000, 1000
NT = (((1,), (1,)), ((), ()))
NN = (((1,), (0,)), ((), ()))


def dot(a, b, dims):
    return lax.dot_general(a, b, dims, preferred_element_type=jnp.float32)


def swap(value, axis):
    return lax.ppermute(value, axis, [(i, i ^ 1) for i in range(lax.axis_size(axis))])


def routed(value, route, backwards=False):
    count = lax.axis_size("ctx")
    pairs = [(c, route(c)) for c in range(count) if route(c) < count]
    if backwards:
        pairs = [(b, a) for a, b in pairs]
    return lax.ppermute(value, "ctx", pairs)


def two_on(c):
    return c + 2


def one_or_three_on(c):
    return c + 1 if c % 2 == 0 else c + 3


def mark_live(tiles, slots, turn, steps, pairs, counts, live):
    def clear(i, _):
        live[i] = 0
        return _

    lax.fori_loop(0, WIN * tiles * tiles, clear, 0)
    for b, step in steps:

        def mark(slot, _, b=b, step=step):
            q_at, k_at = pairs[0, step, 0, slot], pairs[0, step, 1, slot]
            if tiles == 2:
                q_at, k_at = (q_at + turn) % 2, (k_at + turn) % 2
            live[(b * tiles + k_at) * tiles + q_at] = 1
            return _

        lax.fori_loop(0, counts[0, step], mark, 0)


def block_kernel(tiles, group, slots, *refs):
    pairs, counts, q_all, g_all, rows_ref, kv_own, kv_two, kv_core, kv_odd = refs[:9]
    dq_ref, d_own, d_two, d_core, d_odd, live, k_rows, v_rows, k_cols, dk_sum, dv_sum = refs[9:]
    scale = HEAD_DIM**-0.5
    odd = lax.axis_index("ctx") % 2
    block = tiles * TILE
    chunk = 2 * TILE
    steps = enumerate((0, 2, 1 + 2 * odd, 3 - 2 * odd))
    mark_live(tiles, slots, 0, steps, pairs, counts, live)
    for b, ref in enumerate((kv_own, kv_two, kv_core, kv_odd)):
        for t in range(tiles):
            at = pl.ds(b * block + t * TILE, TILE)
            k_rows[at, :] = ref[t, 0]
            v_rows[at, :] = ref[t, 1]
            k_cols[:, at] = ref[t, 0].T
    below = lax.broadcasted_iota(jnp.int32, (TILE, 2 * TILE), 0)
    across = lax.broadcasted_iota(jnp.int32, (TILE, 2 * TILE), 1) % TILE
    causal = below <= across

    for t in range(tiles):
        for pair in range(group // 2):
            first = t == 0 and pair == 0
            cut = pl.ds(pair * 2 * HEAD_DIM, HEAD_DIM), pl.ds((pair * 2 + 1) * HEAD_DIM, HEAD_DIM)
            q_two = jnp.concatenate([q_all[t, :, cut[0]], q_all[t, :, cut[1]]], axis=0)
            g_two = jnp.concatenate([g_all[t, :, cut[0]], g_all[t, :, cut[1]]], axis=0)
            norm = [rows_ref[t, 0, 0, pl.ds(pair * 2 + i, 1), :] for i in range(2)]
            delta = [rows_ref[t, 1, 0, pl.ds(pair * 2 + i, 1), :] for i in range(2)]
            norm = jnp.concatenate(norm, axis=1) * LOG2E
            delta = jnp.concatenate(delta, axis=1)

            def one_chunk(n, dq, t=t, first=first, q_two=q_two, g_two=g_two, norm=norm, delta=delta):
                at = pl.ds(pl.multiple_of(n * chunk, chunk), chunk)
                scores = dot(k_rows[at, :], q_two, NT) * (scale * LOG2E)
                prob_grad = dot(v_rows[at, :], g_two, NT)
                probs, grads = [], []
                for half in range(2):
                    k_at = n * 2 + half
                    part = slice(half * TILE, (half + 1) * TILE)
                    shift = jnp.where(live[k_at * tiles + t] > 0, norm, FAR)
                    power = jnp.where(causal | (k_at != t), scores[part] - shift, -FAR)
                    prob = jnp.exp2(power)
                    probs.append(prob.astype(jnp.bfloat16))
                    grads.append((prob * (prob_grad[part] - delta)).astype(jnp.bfloat16))
                probs = jnp.concatenate(probs, axis=0)
                grads = jnp.concatenate(grads, axis=0)
                dv = dot(probs, g_two, NN)
                dk = dot(grads, q_two, NN)
                if first:
                    dv_sum[at, :] = dv
                    dk_sum[at, :] = dk
                else:
                    dv_sum[at, :] += dv
                    dk_sum[at, :] += dk
                return dq + dot(k_cols[:, at], grads, NN)

            dq = jnp.zeros((HEAD_DIM, 2 * TILE), jnp.float32)
            dq = lax.fori_loop(0, WIN * block // chunk, one_chunk, dq)
            dq = ((dq * scale).T).astype(jnp.bfloat16)
            dq_ref[t, :, cut[0]] = dq[:TILE]
            dq_ref[t, :, cut[1]] = dq[TILE:]

    for b, ref in enumerate((d_own, d_two, d_core, d_odd)):
        for t in range(tiles):
            at = pl.ds(b * block + t * TILE, TILE)
            ref[t, 0] = (dk_sum[at, :] * scale).astype(ref.dtype)
            ref[t, 1] = dv_sum[at, :].astype(ref.dtype)


def pair_kernel(part, group, slots, blocks, n_unused, *refs):
    refs = list(refs)
    mine, pairs, counts, q_mine, q_far, g_mine, g_far, rows_mine, rows_far = refs[:9]
    del refs[:9]
    sources = {}
    for b in blocks:
        sources[b] = tuple(refs[: 3 if b == 0 else 2])
        del refs[: len(sources[b])]
    del refs[:n_unused]
    dq_outs = (refs.pop(0), refs.pop(0))
    outs = {}
    for b in blocks:
        first = refs.pop(0)
        outs[b] = (first.at[0], first.at[1]) if b == 2 else (first, refs.pop(0))
    live, k_cols, prob_all, grad_all = refs[-4:]
    scale = HEAD_DIM**-0.5
    odd = lax.axis_index("ctx") % 2
    block = 2 * TILE
    units = [(t, pair) for t in range(2) for pair in range(group // 2)]
    step_of = (0, 2, 1 + 2 * odd, 3 - 2 * odd)
    mark_live(2, slots, mine[0], [(b, step_of[b]) for b in blocks], pairs, counts, live)

    below = lax.broadcasted_iota(jnp.int32, (TILE, 2 * TILE), 0)
    across = lax.broadcasted_iota(jnp.int32, (TILE, 2 * TILE), 1) % TILE
    causal = below <= across
    sides = ((q_mine, g_mine), (q_far, g_far))

    def heads_of(ref):
        return [ref[:, i * HEAD_DIM : (i + 1) * HEAD_DIM] for i in range(group)]

    q_all = jnp.concatenate([x for q, g in sides for x in heads_of(q)], axis=0)
    g_all = jnp.concatenate([x for q, g in sides for x in heads_of(g)], axis=0)
    far = rows_far[...].astype(jnp.float32)
    far = sum(far[:, part * 3 + i : part * 3 + i + 1] for i in range(3))
    rows = []
    for t, pair in units:
        at = slice(pair * block, (pair + 1) * block)
        norm, delta = [(rows_mine[i, :, at], far[i, :, at])[t] for i in range(2)]
        rows.append((norm * LOG2E, delta))

    for n, b in enumerate(blocks):
        if b == 0:
            k_mine, v_mine, kv_far = sources[b]
            k = jnp.concatenate([k_mine[...], kv_far[0]], axis=0)
            v = jnp.concatenate([v_mine[...], kv_far[1]], axis=0)
        else:
            kv_near, kv_far = sources[b]
            k = jnp.concatenate([kv_near[0], kv_far[0]], axis=0)
            v = jnp.concatenate([kv_near[1], kv_far[1]], axis=0)
        at = slice(n * block, (n + 1) * block)
        k_cols[:, at] = k.T
        for u, (t, pair) in enumerate(units):
            cut = slice(u * block, (u + 1) * block)
            norm, delta = rows[u]
            scores = dot(k, q_all[cut], NT) * (scale * LOG2E)
            prob_grad = dot(v, g_all[cut], NT)
            for k_at in range(2):
                part = slice(k_at * TILE, (k_at + 1) * TILE)
                shift = jnp.where(live[(b * 2 + k_at) * 2 + t] > 0, norm, FAR)
                power = scores[part] - shift
                if b == 0 and k_at == t:
                    power = jnp.where(causal, power, -FAR)
                prob = jnp.exp2(power)
                to = slice(n * block + k_at * TILE, n * block + (k_at + 1) * TILE)
                prob_all[to, cut] = prob.astype(jnp.bfloat16)
                grad_all[to, cut] = (prob * (prob_grad[part] - delta)).astype(jnp.bfloat16)
        dv = dot(prob_all[at, :], g_all, NN)
        dk = dot(grad_all[at, :], q_all, NN) * scale
        for t, out in enumerate(outs[b]):
            part = slice(t * TILE, (t + 1) * TILE)
            out[0] = dk[part].astype(out.dtype)
            out[1] = dv[part].astype(out.dtype)

    for u, (t, pair) in enumerate(units):
        cut = slice(u * block, (u + 1) * block)
        dq = dot(k_cols[...], grad_all[:, cut], NN)
        dq = (dq * scale).T.astype(jnp.bfloat16)
        for i in range(2):
            head = pair * 2 + i
            dq_outs[t][:, head * HEAD_DIM : (head + 1) * HEAD_DIM] = dq[i * TILE : (i + 1) * TILE]


def by_blocks(queries, keys, values, out_grad, log_norm, row_delta, tile_pairs, pair_count):
    heads = lax.axis_size("head")
    rows = queries.shape[0]
    width = queries.shape[1] // heads
    kv_width = keys.shape[1] // heads
    local_kv = kv_width // HEAD_DIM
    group = width // kv_width
    tiles = heads * rows // TILE
    per = rows // TILE

    def spread(x, split_at):
        return lax.all_to_all(x, "head", split_axis=split_at, concat_axis=0)

    kv_own = spread(jnp.stack([keys, values]).reshape(2, rows, heads, kv_width), 2)
    kv_own = jnp.swapaxes(kv_own.reshape(heads, 2, per, TILE, kv_width), 1, 2)
    kv_own = kv_own.reshape(tiles, 2, TILE, kv_width)
    q_all = spread(queries.reshape(rows, heads, width), 1).reshape(tiles, TILE, width)
    g_all = spread(out_grad.reshape(rows, heads, width), 1).reshape(tiles, TILE, width)
    small = jnp.stack([log_norm.T, row_delta.T]).reshape(2, heads, local_kv, group, rows)
    small = spread(small, 1).reshape(heads, 2, local_kv, group, per, TILE)
    small = jnp.moveaxis(small, 4, 1).reshape(tiles, 2, local_kv, group, TILE)

    kv_two = routed(kv_own, two_on)
    kv_odd = routed(kv_own, one_or_three_on)
    kv_core = swap(kv_two, "ctx")

    kv_spec = pl.BlockSpec((tiles, 2, TILE, HEAD_DIM), lambda h, *_: (0, 0, 0, h))
    q_spec = pl.BlockSpec((tiles, TILE, group * HEAD_DIM), lambda h, *_: (0, 0, h))
    small_spec = pl.BlockSpec((tiles, 2, 1, group, TILE), lambda h, *_: (0, 0, h, 0, 0))
    keys_all = WIN * tiles * TILE
    kinds = (jnp.float32, jnp.float32, jnp.bfloat16, jnp.bfloat16)
    dq, d_own, d_two, d_core, d_odd = pl.pallas_call(
        functools.partial(block_kernel, tiles, group, tile_pairs.shape[2]),
        out_shape=[jax.ShapeDtypeStruct(q_all.shape, jnp.bfloat16)]
        + [jax.ShapeDtypeStruct(kv_own.shape, t) for t in kinds],
        grid_spec=pltpu.PrefetchScalarGridSpec(
            num_scalar_prefetch=2,
            grid=(local_kv,),
            in_specs=[q_spec, q_spec, small_spec] + [kv_spec] * 4,
            out_specs=[q_spec] + [kv_spec] * 4,
            scratch_shapes=[
                pltpu.SMEM((WIN * tiles * tiles,), jnp.int32),
                pltpu.VMEM((keys_all, HEAD_DIM), jnp.bfloat16),
                pltpu.VMEM((keys_all, HEAD_DIM), jnp.bfloat16),
                pltpu.VMEM((HEAD_DIM, keys_all), jnp.bfloat16),
                pltpu.VMEM((keys_all, HEAD_DIM), jnp.float32),
                pltpu.VMEM((keys_all, HEAD_DIM), jnp.float32),
            ],
        ),
        compiler_params=pltpu.CompilerParams(vmem_limit_bytes=48 * 1024 * 1024),
        name="block_grads",
    )(jnp.swapaxes(tile_pairs, 2, 3), pair_count, q_all, g_all, small, kv_own, kv_two, kv_core, kv_odd)
    d_all = home(d_own, d_two, d_core, d_odd)
    dq = lax.all_to_all(dq.reshape(heads, rows, width), "head", split_axis=0, concat_axis=1)
    d_all = jnp.swapaxes(d_all.reshape(heads, per, 2, TILE, kv_width), 1, 2)
    d_all = d_all.reshape(heads, 2, rows, kv_width)
    d_all = lax.all_to_all(d_all, "head", split_axis=0, concat_axis=2).reshape(2, *keys.shape)
    return dq.reshape(queries.shape), d_all[0], d_all[1]


def home(d_own, d_two, d_core, d_odd):
    from_odd = routed(d_odd, one_or_three_on, backwards=True)
    d_two = d_two + swap(d_core, "ctx").astype(jnp.float32)
    from_two = routed(d_two.astype(jnp.bfloat16), two_on, backwards=True)
    total = d_own + from_odd.astype(jnp.float32) + from_two.astype(jnp.float32)
    return total.astype(jnp.bfloat16)


def then(value, *before):
    return lax.optimization_barrier((value, *before))[0]


def pack_kernel(heads, mine, q_far, g_far, norm, delta, *outs):
    *parts, rows = outs
    size = parts[0].shape[2]
    tile = q_far.shape[0]
    for p, part in enumerate(parts):
        cut = slice(p * size, (p + 1) * size)
        part[0, :tile] = q_far[:, cut]
        part[1, :tile] = g_far[:, cut]
    for i, ref in enumerate((norm, delta)):
        both = ref[...]
        low_side = mine[0] == 0
        own = jnp.where(low_side, both[:heads], both[heads:])
        other = jnp.where(low_side, both[heads:], both[:heads])
        high = other.astype(jnp.bfloat16)
        rest = other - high.astype(jnp.float32)
        middle = rest.astype(jnp.bfloat16)
        low = (rest - middle.astype(jnp.float32)).astype(jnp.bfloat16)
        for h in range(heads):
            rows[i, :, h * tile : (h + 1) * tile] = own[h : h + 1]
        per = size // tile
        pad = [jnp.zeros((16 - 3 * len(parts), tile), jnp.float32)]
        for at in range(per):
            heads_at = [at + p * per for p in range(len(parts))]
            three = [x[h : h + 1].astype(jnp.float32) for h in heads_at for x in (high, middle, low)]
            block = jnp.concatenate(three + pad, axis=0).astype(jnp.bfloat16)
            parts[0][i, tile:, at * tile : (at + 1) * tile] = block


def fill_kernel(mine, got, before, half):
    half[...] = got[...]


def after(value, *before):
    return lax.optimization_barrier((value, *before))[0]


def touch_kernel(x_ref, y_ref, mark):
    mark[0] = 1


def touch(x, cost):
    return pl.pallas_call(
        touch_kernel,
        out_shape=jax.ShapeDtypeStruct(x.shape, x.dtype),
        in_specs=[pl.BlockSpec(memory_space=pl.ANY)],
        out_specs=pl.BlockSpec(memory_space=pl.ANY),
        input_output_aliases={0: 0},
        scratch_shapes=[pltpu.SMEM((1,), jnp.int32)],
        cost_estimate=pl.CostEstimate(flops=cost, bytes_accessed=1, transcendentals=0),
        name="arrived",
    )(x)


def by_pairs(queries, keys, values, out_grad, log_norm, row_delta, tile_pairs, pair_count):
    mine = lax.axis_index("head")
    rows = queries.shape[0]
    width = queries.shape[1] // 2
    kv_width = keys.shape[1] // 2
    local_kv = kv_width // HEAD_DIM
    group = width // kv_width
    kvs = local_kv // PARTS
    wide = group * HEAD_DIM
    lists = (mine.reshape(1), jnp.swapaxes(tile_pairs, 2, 3), pair_count)

    def cut(x, side):
        size = x.shape[1] // 2
        return lax.dynamic_slice_in_dim(x, side * size, size, 1)

    kv_near = jnp.stack([cut(keys, mine), cut(values, mine)])
    kv_far = swap(jnp.stack([cut(keys, 1 - mine), cut(values, 1 - mine)]), "head")
    kv_far = touch(kv_far, TOUCH_COST)
    pack_spec = pl.BlockSpec((rows, width), lambda i, mine: (0, 1 - mine[0]))
    whole_spec = pl.BlockSpec((2 * local_kv * group, rows), lambda i, mine: (0, 0))
    packed = [(2, rows + (16 if part == 0 else 0), kvs * wide) for part in range(PARTS)]
    *qg_send, small = pl.pallas_call(
        functools.partial(pack_kernel, local_kv * group),
        out_shape=[pltpu.HBM(s, jnp.bfloat16) for s in packed]
        + [jax.ShapeDtypeStruct((2, 1, width), jnp.float32)],
        grid_spec=pltpu.PrefetchScalarGridSpec(
            num_scalar_prefetch=1,
            grid=(1,),
            in_specs=[pack_spec, pack_spec, whole_spec, whole_spec],
            out_specs=[pl.BlockSpec(s, lambda i, mine: (0, 0, 0)) for s in packed + [(2, 1, width)]],
        ),
        compiler_params=pltpu.CompilerParams(vmem_limit_bytes=SMALL_LIMIT),
        cost_estimate=pl.CostEstimate(flops=PACK_COST, bytes_accessed=1, transcendentals=0),
        name="pack_sends",
    )(lists[0], queries, out_grad, log_norm.T, row_delta.T)
    qg_far = [swap(x, "head") for x in qg_send]
    near_two, near_odd = routed(kv_near, two_on), routed(after(kv_near, kv_far), one_or_three_on)
    far_two, far_odd = routed(kv_far, two_on), routed(kv_far, one_or_three_on)
    near_core = swap(near_two, "ctx")

    def attend(part, blocks, sources, before, cost):
        first = part * kvs

        def at_mine(h, mine, *_):
            return (0, mine[0] * local_kv + first + h)

        q_own = pl.BlockSpec((rows, wide), at_mine)
        k_own = pl.BlockSpec((rows, HEAD_DIM), at_mine)
        far = lambda i: pl.BlockSpec((None, rows, wide), lambda h, *_: (i, 0, h))
        kv_spec = pl.BlockSpec((2, rows, HEAD_DIM), lambda h, *_: (0, 0, first + h))
        args = [queries, qg_far[part], out_grad, qg_far[part], small, qg_far[0]]
        specs = [
            q_own,
            far(0),
            q_own,
            far(1),
            pl.BlockSpec((2, 1, wide), lambda h, *_: (0, 0, first + h)),
            pl.BlockSpec((2, 16, wide), lambda h, *_: (0, rows // 16, h)),
        ]
        for b in blocks:
            args += sources[b]
            specs += [k_own, k_own, kv_spec] if b == 0 else [kv_spec, kv_spec]
        dq_shapes = [queries.shape, (rows, width)]
        outs = [pltpu.HBM(s, jnp.bfloat16) for s in dq_shapes]
        out_specs = [q_own, pl.BlockSpec((rows, wide), lambda h, *_: (0, first + h))]
        kinds = (jnp.float32, jnp.float32, jnp.bfloat16, jnp.bfloat16)
        both_spec = pl.BlockSpec((2, 2, rows, HEAD_DIM), lambda h, *_: (0, 0, 0, first + h))
        for b in blocks:
            if b == 2:
                outs.append(pltpu.HBM((2, 2, rows, kv_width), kinds[b]))
                out_specs.append(both_spec)
            else:
                outs += [pltpu.HBM((2, rows, kv_width), kinds[b])] * 2
                out_specs += [kv_spec] * 2
        alias, n_args = {}, len(args)
        if before is not None:
            for i, array in enumerate(before):
                alias[len(lists) + len(args)] = i
                args.append(array)
        specs += [pl.BlockSpec(memory_space=pl.ANY)] * (len(args) - n_args)
        keys_all = len(blocks) * 2 * TILE
        return pl.pallas_call(
            functools.partial(
                pair_kernel,
                part,
                group,
                tile_pairs.shape[2],
                blocks,
                len(args) - n_args,
            ),
            out_shape=outs,
            grid_spec=pltpu.PrefetchScalarGridSpec(
                num_scalar_prefetch=3,
                grid=(kvs,),
                in_specs=specs,
                out_specs=out_specs,
                scratch_shapes=[
                    pltpu.SMEM((WIN * 4,), jnp.int32),
                    pltpu.VMEM((HEAD_DIM, keys_all), jnp.bfloat16),
                    pltpu.VMEM((keys_all, 2 * group * TILE), jnp.bfloat16),
                    pltpu.VMEM((keys_all, 2 * group * TILE), jnp.bfloat16),
                ],
            ),
            input_output_aliases=alias,
            compiler_params=pltpu.CompilerParams(vmem_limit_bytes=VMEM_LIMIT),
            cost_estimate=pl.CostEstimate(flops=cost, bytes_accessed=1, transcendentals=0),
            name="grads_" + "".join(map(str, blocks)) + "_part" + str(part),
        )(*lists, *args)

    sources = {
        0: (keys, values, kv_far),
        1: (near_two, far_two),
        2: (near_core, swap(far_two, "ctx")),
        3: (near_odd, far_odd),
    }
    def wide_sum(*terms):
        return sum(x.astype(jnp.float32) for x in terms).astype(jnp.bfloat16)

    blocks = (0, 1, 2, 3)
    first = attend(0, blocks, sources, None, FIRST_COST)
    dq_near, dq_far, *sums = attend(1, blocks, sources, first, SECOND_COST)
    own_n, own_f, two_n, two_f, core, odd_n, odd_f = sums
    core = swap(core, "ctx")
    dq_far = swap(dq_far, "head")
    far_odd = routed(odd_f, one_or_three_on, backwards=True)
    far_two = wide_sum(two_f, core[1])
    odd_n, two_n = after((odd_n, two_n), far_two)
    far_two = routed(far_two, two_on, backwards=True)
    near_odd = routed(odd_n, one_or_three_on, backwards=True)
    near_two = routed(wide_sum(two_n, core[0]), two_on, backwards=True)
    far = swap(wide_sum(after(own_f, dq_far), far_odd, far_two), "head")
    near = wide_sum(own_n, near_odd, near_two)

    def whole(near, far):
        return jnp.where(mine == 0, jnp.concatenate(near + far, -1), jnp.concatenate(far + near, -1))

    both = whole([near], [far])
    half = pl.BlockSpec((rows, width), lambda i, mine: (0, 1 - mine[0]))
    dq = pl.pallas_call(
        fill_kernel,
        out_shape=jax.ShapeDtypeStruct(queries.shape, jnp.bfloat16),
        grid_spec=pltpu.PrefetchScalarGridSpec(
            num_scalar_prefetch=1,
            grid=(1,),
            in_specs=[pl.BlockSpec((rows, width), lambda i, mine: (0, 0))]
            + [pl.BlockSpec(memory_space=pl.ANY)],
            out_specs=half,
        ),
        input_output_aliases={2: 0},
        compiler_params=pltpu.CompilerParams(vmem_limit_bytes=SMALL_LIMIT),
        cost_estimate=pl.CostEstimate(flops=DQ_COST, bytes_accessed=1, transcendentals=0),
        name="fill_in",
    )(lists[0], dq_far, dq_near)
    return dq, both[0], both[1]


def per_device(queries, keys, values, out_grad, log_norm, row_delta, tile_pairs, pair_count):
    heads = lax.axis_size("head")
    local_kv = keys.shape[1] // heads // HEAD_DIM
    group = queries.shape[1] // keys.shape[1]
    paired = heads == 2 and queries.shape[0] == TILE and local_kv % PARTS == 0 and group % 2 == 0
    form = by_pairs if paired else by_blocks
    return form(queries, keys, values, out_grad, log_norm, row_delta, tile_pairs, pair_count)


def solution(mesh):
    rows = P(("ctx", "head"), None)
    return jax.shard_map(
        per_device,
        mesh=mesh,
        in_specs=(rows,) * 6 + (P("ctx", None, None, None), P("ctx", None)),
        out_specs=(rows,) * 3,
        check_vma=False,
    )
```
